32 devices in a mesh: ctx: 8 (over z, y), head: 4 (over x, core).
Axes of the slice: x: 2, y: 2, z: 4, core: 2. Of those that a mesh axis runs over, the one named last changes fastest.
Arguments:
- layer_input: bfloat16 [2048, 2048], P('ctx', 'head'), may hold values from -6 to 6
- queries: bfloat16 [2048, 1024], P('ctx', 'head'), may hold values from -6 to 6
- keys: bfloat16 [2048, 512], P('ctx', 'head'), may hold values from -6 to 6
- values: bfloat16 [2048, 512], P('ctx', 'head'), may hold values from -6 to 6
- result_cotangent: bfloat16 [2048, 1024], P('ctx', 'head'), may hold values from -0.3125 to 0.3125
- log_decay: float32 [4, 2048], P('head', 'ctx'), may hold values from -2 to 0
Outputs:
- weight_k_grad: bfloat16 [2048, 512], P('ctx', 'head')
- weight_v_grad: bfloat16 [2048, 512], P('ctx', 'head')
The draws below stay inside these ranges and needn't reach their ends.
All inputs are finite; a program needn't handle non-finite values.
Results may differ from the reference program's by a relative error of at most 0.0057.
Values may be sent and summed in bfloat16 or wider, within the bound.
A program may use at most 64 MiB of HBM per device.

```python
import math
import jax
import jax.numpy as jnp
from jax import lax

D = 2048
HQ = 8
HK = 4
E = 128
WINDOW = 256
TOK_DEV = 256
TOKENS = 2048


def pair_draw(key):
    base = jax.random.fold_in(key, 7)
    key_q, key_k = jax.random.split(base, 2)
    query_draw = jax.random.truncated_normal(key_q, -6.0, 6.0, (TOKENS, HQ * E), jnp.float32)
    key_draw = jax.random.truncated_normal(key_k, -6.0, 6.0, (TOKENS, HK * E), jnp.float32)
    return (query_draw, key_draw)


def draw_queries(key, part):
    return pair_draw(key)[0].astype(jnp.bfloat16)


def draw_keys(key, part):
    return pair_draw(key)[1].astype(jnp.bfloat16)


def draw_log_decay(key, part):
    base = jax.random.fold_in(key, 11)
    key_order, key_slow, key_fast, key_device, key_rough, key_spot, dropout_key_seed = jax.random.split(base, 7)
    order = jax.random.permutation(key_order, HK)
    fast_count = HK // 2
    fast_heads = (order < fast_count)[:, None]
    slow_rate = jax.random.uniform(key_slow, (HK, 1), jnp.float32, 0.2, 0.4) / TOKENS
    fast_rate = jax.random.uniform(key_fast, (HK, 1), jnp.float32, 0.02, 0.04)
    arrival_frequency = jnp.where(fast_heads, fast_rate, slow_rate)
    block_count = TOKENS // TOK_DEV
    shard_among_cards = jnp.exp(jax.random.uniform(key_device, (HK, block_count), jnp.float32, 0.0, math.log(2.5)))
    shard_among_cards = jnp.repeat(shard_among_cards, TOK_DEV, axis=1)
    boundary_perturbation = jax.random.uniform(key_rough, (HK, TOKENS), jnp.float32, 0.5, 1.5)
    spots = jax.random.randint(key_spot, (HK, 2), 0, TOKENS)
    discarded_arrivals = jnp.log(1.0 - jax.random.uniform(dropout_key_seed, (HK, 2), jnp.float32, 0.2, 0.4))
    paired_arrivals = jnp.arange(TOKENS)[None, None, :] == spots[:, :, None]
    clustered_arrivals = jnp.sum(jnp.where(paired_arrivals, discarded_arrivals[:, :, None], 0.0), axis=1)
    return (-arrival_frequency * shard_among_cards * boundary_perturbation + clustered_arrivals).astype(jnp.float32)


def raised(drawn, key, source, target, parts, factor):
    owner, partner = [(jnp.arange(drawn.shape[axis_at]) // (drawn.shape[axis_at] // parts)).reshape([-1 if axis == axis_at else 1 for axis in range(drawn.ndim)]) for axis_at in (source, target)]
    chosen = jax.random.permutation(key, parts)[partner]
    strong = (owner == chosen) | (owner == (partner + parts // 2) % parts)
    return jnp.where(strong, factor * drawn, drawn)


def block_levels(stream_key, extent, cuts, low, largest):
    level = 1.0
    for axis_at, shards_of in cuts:
        draws = jax.random.uniform(jax.random.fold_in(jax.random.fold_in(stream_key, 6), axis_at), (shards_of,), jnp.float32, low / len(cuts), largest / len(cuts))
        level = level * jnp.repeat(jnp.exp(draws), extent[axis_at] // shards_of).reshape((-1,) + (1,) * (len(extent) - 1 - axis_at))
    return level


def gaussian(rng, dims, deviation, reach, pieces=(), kind=jnp.bfloat16):
    result = jax.random.normal(rng, dims, jnp.float32) * deviation
    if len(pieces) > 0:
        result = block_levels(rng, dims, pieces, -0.22, 0.18) * result
    return jnp.clip(result, min=-reach, max=reach).astype(kind)


def bell_draw_with(rng, dims, width, bound, cuts, heavy, kind=jnp.bfloat16):
    array = width * jax.random.normal(rng, dims, jnp.float32)
    if cuts:
        array = array * block_levels(rng, dims, cuts, -0.22, 0.18)
    return jnp.clip(raised(array, jax.random.fold_in(rng, 3), *heavy), -bound, bound).astype(kind)


def setup_inputs(seed: int = 0) -> dict:
    splits = jax.random.split(jax.random.key(seed), 7)
    return {
        "layer_input": bell_draw_with(splits[0], (TOKENS, D), 1.0, 6.0, ((0, 8), (1, 4)), (0, 1, 8, 2.0)),
        "queries": draw_queries(jax.random.fold_in(splits[6], 71), 0),
        "keys": draw_keys(jax.random.fold_in(splits[6], 71), 0),
        "values": gaussian(splits[3], (TOKENS, HK * E), 1.0, 6.0, ((0, 8), (1, 4))),
        "result_cotangent": gaussian(splits[4], (TOKENS, HQ * E), 0.02, 0.3125, ((0, 8), (1, 4))),
        "log_decay": draw_log_decay(jax.random.fold_in(splits[6], 71), 0),
    }


neg_fill = -1e+30

def rounded(value):
    return lax.optimization_barrier(value.astype(jnp.bfloat16)).astype(jnp.float32)

def band_terms(q_rows, h_rows, k_rows, v_rows, query_pos, key_pos):
    factor = 1.0 / math.sqrt(E)
    scores = jnp.einsum('tgrd,jgd->grtj', q_rows, k_rows) * factor
    offset = query_pos[:, None] - key_pos[None, :]
    inside = (offset >= 0) & (offset < WINDOW) & (key_pos[None, :] >= 0)
    scores = jnp.where(inside, scores, neg_fill)
    row_max = lax.optimization_barrier(jnp.max(scores, axis=3, keepdims=True))
    expo = jnp.exp(scores - row_max)
    attend = expo / lax.optimization_barrier(jnp.sum(expo, axis=3, keepdims=True))
    attend_low = rounded(attend)
    dprob = jnp.einsum('tgrd,jgd->grtj', h_rows, v_rows)
    row_delta = lax.optimization_barrier(jnp.sum(attend * dprob, axis=3, keepdims=True))
    dscore = rounded(attend * (dprob - row_delta))
    key_part = jnp.einsum('grtj,tgrd->jgd', dscore, q_rows) * factor
    value_part = jnp.einsum('grtj,tgrd->jgd', attend_low, h_rows)
    return (key_part, value_part)

def reference(layer_input, queries, keys, values, result_cotangent, log_decay):
    group_size = HQ // HK
    block_count = TOKENS // TOK_DEV
    lin_scale = 1.0 / (32 * E)
    q_all = queries.astype(jnp.float32).reshape(TOKENS, HK, group_size, E)
    h_all = (result_cotangent * 0.5).astype(jnp.float32).reshape(TOKENS, HK, group_size, E)
    k_all = keys.astype(jnp.float32).reshape(TOKENS, HK, E)
    v_all = values.astype(jnp.float32).reshape(TOKENS, HK, E)
    log_sums = jnp.cumsum(log_decay.astype(jnp.float32).reshape(HK, block_count, TOK_DEV), axis=2)

    def summary(block_index):
        row_start = (block_index * TOK_DEV).astype(jnp.int32)
        q_block = lax.dynamic_slice_in_dim(q_all, row_start, TOK_DEV, 0)
        h_block = lax.dynamic_slice_in_dim(h_all, row_start, TOK_DEV, 0)
        sums_block = log_sums[:, block_index]
        weighted = rounded(jnp.exp(sums_block).T[:, :, None, None] * h_block)
        grad_block = jnp.einsum('tgrd,tgre->gde', q_block, weighted) * lin_scale
        return (grad_block, jnp.exp(sums_block[:, -1]))
    block_grads, block_decays = lax.map(summary, jnp.arange(block_count, dtype=jnp.int32))

    def backward_step(incoming, inputs):
        grad_block, decay_block = inputs
        return (grad_block + decay_block[:, None, None] * incoming, incoming)
    _, carries = lax.scan(backward_step, jnp.zeros((HK, E, E), jnp.float32), (block_grads, block_decays), reverse=True)
    q_pad = jnp.pad(q_all, ((WINDOW, WINDOW), (0, 0), (0, 0), (0, 0)))
    h_pad = jnp.pad(h_all, ((WINDOW, WINDOW), (0, 0), (0, 0), (0, 0)))
    k_pad = jnp.pad(k_all, ((WINDOW, WINDOW), (0, 0), (0, 0)))
    v_pad = jnp.pad(v_all, ((WINDOW, WINDOW), (0, 0), (0, 0)))

    def block_work(inputs):
        block_index, incoming = inputs
        row_start = (block_index * TOK_DEV).astype(jnp.int32)
        own_q = lax.dynamic_slice_in_dim(q_pad, row_start + WINDOW, TOK_DEV, 0)
        own_h = lax.dynamic_slice_in_dim(h_pad, row_start + WINDOW, TOK_DEV, 0)
        own_k = lax.dynamic_slice_in_dim(k_pad, row_start, TOK_DEV + WINDOW, 0)
        own_v = lax.dynamic_slice_in_dim(v_pad, row_start, TOK_DEV + WINDOW, 0)
        query_pos = row_start + jnp.arange(TOK_DEV, dtype=jnp.int32)
        key_pos = row_start - WINDOW + jnp.arange(TOK_DEV + WINDOW, dtype=jnp.int32)
        win_k, win_v = band_terms(own_q, own_h, own_k, own_v, query_pos, key_pos)
        next_q = lax.dynamic_slice_in_dim(q_pad, row_start + TOK_DEV + WINDOW, WINDOW, 0)
        next_h = lax.dynamic_slice_in_dim(h_pad, row_start + TOK_DEV + WINDOW, WINDOW, 0)
        next_k = lax.dynamic_slice_in_dim(k_pad, row_start + TOK_DEV, 2 * WINDOW, 0)
        next_v = lax.dynamic_slice_in_dim(v_pad, row_start + TOK_DEV, 2 * WINDOW, 0)
        next_qpos = row_start + TOK_DEV + jnp.arange(WINDOW, dtype=jnp.int32)
        next_kpos = row_start + TOK_DEV - WINDOW + jnp.arange(2 * WINDOW, dtype=jnp.int32)
        edge_k, edge_v = band_terms(next_q, next_h, next_k, next_v, next_qpos, next_kpos)
        zero_rows = jnp.zeros((TOK_DEV - WINDOW, HK, E), jnp.float32)
        win_k = win_k[WINDOW:] + jnp.concatenate([zero_rows, edge_k[:WINDOW]], axis=0)
        win_v = win_v[WINDOW:] + jnp.concatenate([zero_rows, edge_v[:WINDOW]], axis=0)
        k_block = own_k[WINDOW:]
        v_block = own_v[WINDOW:]
        sums_block = log_sums[:, block_index]
        row_after = lax.broadcasted_iota(jnp.int32, (TOK_DEV, TOK_DEV), 0)
        row_before = lax.broadcasted_iota(jnp.int32, (TOK_DEV, TOK_DEV), 1)
        mixing = jnp.exp(jnp.where(row_after >= row_before, sums_block[:, :, None] - sums_block[:, None, :], neg_fill))
        key_mix = rounded(mixing[:, None] * jnp.einsum('tgrd,jgd->grtj', own_h, v_block))
        value_mix = rounded(mixing[:, None] * jnp.einsum('tgrd,jgd->grtj', own_q, k_block))
        lin_k = jnp.einsum('grtj,tgrd->jgd', key_mix, own_q) * lin_scale
        lin_v = jnp.einsum('grtj,tgrd->jgd', value_mix, own_h) * lin_scale
        tail_decay = jnp.exp(sums_block[:, -1:] - sums_block).T[:, :, None]
        lin_k = lin_k + tail_decay * jnp.einsum('tgj,gij->tgi', v_block, incoming, precision=lax.Precision.HIGHEST)
        lin_v = lin_v + tail_decay * jnp.einsum('tgi,gij->tgj', k_block, incoming, precision=lax.Precision.HIGHEST)
        key_grad = (lin_k + win_k).astype(jnp.bfloat16).reshape(TOK_DEV, HK * E)
        value_grad = (lin_v + win_v).astype(jnp.bfloat16).reshape(TOK_DEV, HK * E)
        return (key_grad, value_grad)
    key_blocks, content_tiles = lax.map(block_work, (jnp.arange(block_count, dtype=jnp.int32), carries))
    key_grad = key_blocks.reshape(TOKENS, HK * E)
    value_grad = content_tiles.reshape(TOKENS, HK * E)
    weight_k_grad = jnp.dot(layer_input.T, key_grad, preferred_element_type=jnp.float32).astype(jnp.bfloat16)
    weight_v_grad = jnp.dot(layer_input.T, value_grad, preferred_element_type=jnp.float32).astype(jnp.bfloat16)
    return (weight_k_grad, weight_v_grad)
```

```python
import functools

import jax
import jax.numpy as jnp
from jax import lax
from jax.experimental import pallas as pl
from jax.experimental.pallas import tpu as pltpu
from jax.sharding import PartitionSpec as P

E = 128
WINDOW = 256


neg_fill = -1e30


def entering(array, axis, combine, identity):
    size, position = (lax.axis_size(axis), lax.axis_index(axis))
    everything = jax.tree.map(lambda part: lax.all_gather(part, axis), array)
    start = jax.tree.map(
        lambda part, zero: jnp.broadcast_to(jnp.asarray(zero, part.dtype), part.shape),
        array,
        identity,
    )

    def turn(k, before):
        at = size - 1 - k
        reached = at > position
        new = combine(before, jax.tree.map(lambda part: part[at], everything))
        return jax.tree.map(lambda a, b: jnp.where(reached, a, b), new, before)

    return lax.fori_loop(0, size, turn, start)


def shifted(value, axis, steps):
    count = lax.axis_size(axis)
    leading, last = (max(0, -steps), min(count, count - steps))
    return lax.ppermute(value, axis, [(source, source + steps) for source in range(leading, last)])


def band_grads(q_block, h_block, key_rows, value_rows, query_pos, key_pos):
    head_dim = key_rows.shape[1]
    group_size = q_block.shape[1] // head_dim
    row_count = q_block.shape[0]
    q_heads = q_block.reshape(row_count, group_size, head_dim)
    h_heads = h_block.reshape(row_count, group_size, head_dim)
    factor = head_dim ** (-0.5)
    scores = (
        jnp.einsum("trd,jd->rtj", q_heads, key_rows, preferred_element_type=jnp.float32) * factor
    )
    offset = query_pos[:, None] - key_pos[None, :]
    inside = (offset >= 0) & (offset < WINDOW) & (key_pos[None, :] >= 0)
    scores = jnp.where(inside[None], scores, neg_fill)
    row_max = jnp.max(scores, axis=2, keepdims=True)
    expo = jnp.exp(scores - row_max)
    attend = expo / jnp.sum(expo, axis=2, keepdims=True)
    attend_low = attend.astype(jnp.bfloat16)
    dprob = jnp.einsum("trd,jd->rtj", h_heads, value_rows, preferred_element_type=jnp.float32)
    row_delta = jnp.sum(attend * dprob, axis=2, keepdims=True)
    dscore = (attend * (dprob - row_delta)).astype(jnp.bfloat16)
    key_part = (
        jnp.einsum("rtj,trd->jd", dscore, q_heads, preferred_element_type=jnp.float32) * factor
    )
    value_part = jnp.einsum("rtj,trd->jd", attend_low, h_heads, preferred_element_type=jnp.float32)
    return (key_part, value_part)


def linear_terms(q_block, h_block, key_rows, value_rows, log_rates, lin_scale):
    head_dim = key_rows.shape[1]
    group_size = q_block.shape[1] // head_dim
    length = q_block.shape[0]
    q_heads = q_block.reshape(length, group_size, head_dim)
    h_heads = h_block.reshape(length, group_size, head_dim)
    row_after = lax.broadcasted_iota(jnp.int32, (length, length), 0)
    row_before = lax.broadcasted_iota(jnp.int32, (length, length), 1)
    log_sums = jnp.sum(jnp.where(row_after >= row_before, log_rates[None, :], 0.0), axis=1)
    mixing = jnp.exp(
        jnp.where(row_after >= row_before, log_sums[:, None] - log_sums[None, :], neg_fill)
    )
    key_mix = (
        mixing[None]
        * jnp.einsum("trd,jd->rtj", h_heads, value_rows, preferred_element_type=jnp.float32)
    ).astype(jnp.bfloat16)
    value_mix = (
        mixing[None]
        * jnp.einsum("trd,jd->rtj", q_heads, key_rows, preferred_element_type=jnp.float32)
    ).astype(jnp.bfloat16)
    key_part = (
        jnp.einsum("rtj,trd->jd", key_mix, q_heads, preferred_element_type=jnp.float32) * lin_scale
    )
    value_part = (
        jnp.einsum("rtj,trd->jd", value_mix, h_heads, preferred_element_type=jnp.float32)
        * lin_scale
    )
    weighted = (jnp.exp(log_sums)[:, None, None] * h_heads).astype(jnp.bfloat16)
    block_grad = (
        jnp.einsum("trd,tre->de", q_heads, weighted, preferred_element_type=jnp.float32) * lin_scale
    )
    return (
        key_part,
        value_part,
        block_grad,
        jnp.exp(log_sums[-1]),
        jnp.exp(log_sums[-1] - log_sums),
    )


def compose(earlier, later):
    return (later[0] * earlier[0], later[0][:, None, None] * earlier[1] + later[1])


def on_device(layer_input, queries, keys, values, result_cotangent, log_decay):
    length = queries.shape[0]
    head_dim = E
    lin_scale = 1.0 / (32 * head_dim)
    halves = result_cotangent * 0.5
    row_start = lax.axis_index("ctx") * length
    query_pos = row_start + jnp.arange(length, dtype=jnp.int32)
    key_pos = row_start - WINDOW + jnp.arange(length + WINDOW, dtype=jnp.int32)
    linear_parts = [linear_terms(queries, halves, keys, values, log_decay[0], lin_scale)]
    decays = jnp.stack([part[3] for part in linear_parts])
    block_grads = jnp.stack([part[2] for part in linear_parts])
    identity = (jnp.ones_like(decays), jnp.zeros_like(block_grads))
    _, incoming = entering((decays, block_grads), "ctx", compose, identity)
    preceding_keys, prior_v = shifted((keys, values), "ctx", 1)
    full_k = jnp.concatenate([preceding_keys, keys], axis=0)
    full_v = jnp.concatenate([prior_v, values], axis=0)
    band_parts = [band_grads(queries, halves, full_k, full_v, query_pos, key_pos)]
    win_k = jnp.concatenate([part[0] for part in band_parts], axis=1)
    win_v = jnp.concatenate([part[1] for part in band_parts], axis=1)
    back_k, back_v = shifted((win_k[:WINDOW], win_v[:WINDOW]), "ctx", -1)
    win_k = win_k[WINDOW:]
    win_v = win_v[WINDOW:]
    zero_rows = jnp.zeros((length - WINDOW, win_k.shape[1]), jnp.float32)
    win_k = win_k + jnp.concatenate([zero_rows, back_k], axis=0)
    win_v = win_v + jnp.concatenate([zero_rows, back_v], axis=0)
    state_in = incoming[0]
    tail_decay = linear_parts[0][4][:, None]
    lin_keys = linear_parts[0][0] + tail_decay * jnp.dot(
        values.astype(jnp.float32), state_in.T, precision=lax.Precision.HIGHEST
    )
    lin_values = linear_parts[0][1] + tail_decay * jnp.dot(
        keys.astype(jnp.float32), state_in, precision=lax.Precision.HIGHEST
    )
    key_grad = (lin_keys + win_k).astype(jnp.bfloat16)
    value_grad = (lin_values + win_v).astype(jnp.bfloat16)
    both_grads = jnp.concatenate([key_grad, value_grad], axis=1)
    partial_value = lax.dot_general(
        lax.all_gather(layer_input, "head", axis=1, tiled=True),
        both_grads,
        (((0,), (0,)), ((), ())),
        preferred_element_type=jnp.float32,
    )
    owned = lax.psum_scatter(partial_value, "ctx", scatter_dimension=0, tiled=True)
    key_width = key_grad.shape[1]
    return (owned[:, :key_width].astype(jnp.bfloat16), owned[:, key_width:].astype(jnp.bfloat16))


MESH = pl.DeviceIdType.MESH
F32, BF16 = jnp.float32, jnp.bfloat16


def fits(args, n, heads):
    x, q, k = args[0], args[1], args[2]
    rows = x.shape[1] * heads // n
    return (
        heads == 4
        and n == 2 * heads
        and rows % 128 == 0
        and x.shape[0] == WINDOW
        and k.shape[1] == E
        and q.shape[1] % E == 0
        and x.shape[1] == 2 * rows
    )


def tn(a, b):
    return lax.dot_general(a, b, (((0,), (0,)), ((), ())), preferred_element_type=F32)


def nt(a, b):
    return lax.dot_general(a, b, (((1,), (1,)), ((), ())), preferred_element_type=F32)


def fused_kernel(
    n, m, x_ref, q_ref, k_ref, v_ref, d_ref, ld_ref, ok_ref, ov_ref,
    xall, gall, sall, halo, back_out, back_in, part_k, part_v, state,
    x_send, x_recv, f_send, g_send, g_recv, s_send, s_recv, h_send, h_recv, b_send, b_recv,
):
    length, width = q_ref.shape
    group = width // E
    rows = x_ref.shape[1] // m
    factor = E ** (-0.5)
    lin_scale = 1.0 / (32 * E)
    c, h = lax.axis_index("ctx"), lax.axis_index("head")
    owner = c // m
    sibling = h + 1 - 2 * lax.rem(h, 2)
    across = lax.rem(h + 2, 4)

    def copy(src, dst, send, recv, ctx, head):
        return pltpu.make_async_remote_copy(
            src_ref=src, dst_ref=dst, send_sem=send, recv_sem=recv,
            device_id=(ctx, head), device_id_type=MESH,
        )

    peers = [lax.rem(c + i, n) for i in range(1, n)]
    barrier = pltpu.get_barrier_semaphore()
    for p in peers:
        pl.semaphore_signal(barrier, inc=1, device_id=(p, h), device_id_type=MESH)
    for i in range(1, 4):
        pl.semaphore_signal(
            barrier, inc=1, device_id=(c, lax.rem(h + i, 4)), device_id_type=MESH
        )
    pl.semaphore_wait(barrier, n + 2)

    def halo_copy(i):
        return copy(
            (k_ref, v_ref)[i], halo.at[i], h_send.at[i], h_recv.at[i], lax.rem(c + 1, n), h
        )

    @pl.when(c < n - 1)
    def _():
        halo_copy(0).start()
        halo_copy(1).start()

    @pl.when(c == 0)
    def _():
        halo[...] = jnp.zeros_like(halo)

    def x_copy(j):
        return copy(
            x_ref.at[:, j * rows : (j + 1) * rows], xall.at[c],
            x_send.at[j], x_recv.at[c], h * m + j, h,
        )

    for j in range(m):

        @pl.when(h * m + j == c)
        def _():
            xall[c] = x_ref[:, j * rows : (j + 1) * rows]

        @pl.when(h * m + j != c)
        def _():
            x_copy(j).start()

    after = lax.broadcasted_iota(jnp.int32, (length, length), 0)
    before = lax.broadcasted_iota(jnp.int32, (length, length), 1)
    lower = after >= before
    sums = jnp.sum(jnp.where(lower, ld_ref[...], 0.0), axis=1, keepdims=True)
    sums_row = jnp.sum(jnp.where(after == before, sums, 0.0), axis=0, keepdims=True)
    total = jnp.sum(ld_ref[...], axis=1, keepdims=True)

    grown = jnp.exp(sums)
    qs, hs, grad = [], [], jnp.zeros((E, E), F32)
    for r in range(group):
        qs.append(q_ref[:, r * E : (r + 1) * E])
        hs.append((d_ref[:, r * E : (r + 1) * E].astype(F32) * 0.5).astype(BF16))
        grad += tn(qs[r], (grown * hs[r].astype(F32)).astype(BF16))
    decay = jnp.broadcast_to(jnp.exp(total), (16, E))
    coarse = decay.astype(BF16)
    fine = (decay - coarse.astype(F32)).astype(BF16)
    sall[c, 0:E, :] = (grad * lin_scale).astype(BF16)
    sall[c, E : E + 16, :] = coarse
    sall[c, E + 16 : E + 32, :] = fine

    def state_copy(i):
        return copy(
            sall.at[c], sall.at[c], s_send.at[i], s_recv.at[c], lax.rem(c + n - i, n), h
        )

    for i in range(1, n):

        @pl.when(c - i >= 0)
        def _():
            state_copy(i).start()

    mixing = jnp.exp(jnp.where(lower, sums - sums_row, neg_fill))
    keys, vals = k_ref[...], v_ref[...]
    lin_k = jnp.zeros((length, E), F32)
    lin_v = jnp.zeros((length, E), F32)
    own_s, own_p = [], []
    for r in range(group):
        own_s.append(nt(qs[r], keys))
        own_p.append(nt(hs[r], vals))
        lin_k += tn((mixing * own_p[r]).astype(BF16), qs[r])
        lin_v += tn((mixing * own_s[r]).astype(BF16), hs[r])

    @pl.when(c > 0)
    def _():
        halo_copy(0).wait_recv()
        halo_copy(1).wait_recv()

    old_k, old_v = halo[0], halo[1]
    upper = jnp.logical_and(before > after, c > 0)
    win = [jnp.zeros((length, E), F32) for _ in range(4)]
    for r in range(group):
        s_own = jnp.where(lower, own_s[r] * factor, neg_fill)
        s_old = jnp.where(upper, nt(qs[r], old_k) * factor, neg_fill)
        top = jnp.maximum(
            jnp.max(s_own, axis=1, keepdims=True), jnp.max(s_old, axis=1, keepdims=True)
        )
        e_own, e_old = jnp.exp(s_own - top), jnp.exp(s_old - top)
        inv = 1.0 / (jnp.sum(e_own, axis=1, keepdims=True) + jnp.sum(e_old, axis=1, keepdims=True))
        a_own, a_old = e_own * inv, e_old * inv
        p_old = nt(hs[r], old_v)
        delta = jnp.sum(a_own * own_p[r], axis=1, keepdims=True) + jnp.sum(
            a_old * p_old, axis=1, keepdims=True
        )
        win[0] += tn((a_old * (p_old - delta)).astype(BF16), qs[r])
        win[1] += tn(a_old.astype(BF16), hs[r])
        win[2] += tn((a_own * (own_p[r] - delta)).astype(BF16), qs[r])
        win[3] += tn(a_own.astype(BF16), hs[r])
    back_out[0] = (win[0] * factor).astype(BF16)
    back_out[1] = win[1].astype(BF16)

    def back_copy(i):
        return copy(
            back_out.at[i], back_in.at[i], b_send.at[i], b_recv.at[i], lax.rem(c + n - 1, n), h
        )

    @pl.when(c > 0)
    def _():
        back_copy(0).start()
        back_copy(1).start()

    part_k[...] = lin_k * lin_scale + win[2] * factor
    part_v[...] = lin_v * lin_scale + win[3]

    def forward(slot, i, head):
        return copy(xall.at[slot], xall.at[slot], f_send.at[i], x_recv.at[slot], c, head)

    def arrived(slot):
        return copy(xall.at[slot], xall.at[slot], x_send.at[0], x_recv.at[slot], c, sibling)

    @pl.when(h == owner)
    def _():
        for i in range(n):
            slot = lax.rem(c + i, n)
            if i:
                arrived(slot).wait_recv()
            forward(slot, 2 * i, across).start()
            forward(slot, 2 * i + 1, sibling).start()

    state[...] = jnp.zeros_like(state)
    for i in range(n - 1, 0, -1):

        @pl.when(c + i < n)
        def _():
            slot = lax.rem(c + i, n)
            copy(
                sall.at[slot], sall.at[slot], s_send.at[0], s_recv.at[slot], slot, h
            ).wait_recv()
            kept = sall[slot, E : E + 1, :].astype(F32) + sall[slot, E + 16 : E + 17, :].astype(F32)
            state[...] = kept * state[...] + sall[slot, 0:E, :].astype(F32)

    high = state[...].astype(BF16)
    low = (state[...] - high.astype(F32)).astype(BF16)
    ending = jnp.exp(total - sums)
    part_k[...] += ending * (nt(vals, high) + nt(vals, low))
    part_v[...] += ending * (
        jnp.dot(keys, high, preferred_element_type=F32)
        + jnp.dot(keys, low, preferred_element_type=F32)
    )

    @pl.when(c < n - 1)
    def _():
        back_copy(0).wait_recv()
        back_copy(1).wait_recv()
        part_k[...] += back_in[0].astype(F32)
        part_v[...] += back_in[1].astype(F32)

    gall[c, :, 0:E] = part_k[...].astype(BF16)
    gall[c, :, E : 2 * E] = part_v[...].astype(BF16)

    def g_copy(i):
        return copy(gall.at[c], gall.at[c], g_send.at[i], g_recv.at[c], lax.rem(c + i, n), h)

    for i in range(1, n):
        g_copy(i).start()

    @pl.when(across == owner)
    def _():
        for i in range(n):
            slot = lax.rem(c + i, n)
            arrived(slot).wait_recv()
            forward(slot, i, sibling).start()

    @pl.when(lax.rem(h + owner, 2) == 1)
    def _():
        for i in range(n):
            arrived(lax.rem(c + i, n)).wait_recv()

    acc = jnp.zeros((rows, 2 * E), F32)
    for i in range(n):
        slot = lax.rem(c + i, n)
        if i:
            copy(
                gall.at[slot], gall.at[slot], g_send.at[0], g_recv.at[slot], slot, h
            ).wait_recv()
        acc += tn(xall[slot], gall[slot])
    ok_ref[...] = acc[:, 0:E].astype(BF16)
    ov_ref[...] = acc[:, E : 2 * E].astype(BF16)

    @pl.when(c < n - 1)
    def _():
        halo_copy(0).wait_send()
        halo_copy(1).wait_send()

    @pl.when(c > 0)
    def _():
        back_copy(0).wait_send()
        back_copy(1).wait_send()

    for j in range(m):

        @pl.when(h * m + j != c)
        def _():
            x_copy(j).wait_send()

    for i in range(1, n):

        @pl.when(c - i >= 0)
        def _():
            state_copy(i).wait_send()

    @pl.when(h == owner)
    def _():
        for i in range(n):
            slot = lax.rem(c + i, n)
            forward(slot, 2 * i, across).wait_send()
            forward(slot, 2 * i + 1, sibling).wait_send()

    @pl.when(across == owner)
    def _():
        for i in range(n):
            forward(lax.rem(c + i, n), i, sibling).wait_send()

    for i in range(1, n):
        g_copy(i).wait_send()


def fused(layer_input, queries, keys, values, result_cotangent, log_decay):
    n = lax.axis_size("ctx")
    length, width = layer_input.shape
    rows = width * lax.axis_size("head") // n
    m = width // rows
    dma = pltpu.SemaphoreType.DMA
    shape = jax.ShapeDtypeStruct((rows, E), BF16)
    vmem = pl.BlockSpec(memory_space=pltpu.VMEM)
    return pl.pallas_call(
        functools.partial(fused_kernel, n, m),
        out_shape=(shape, shape),
        in_specs=[vmem] * 6,
        out_specs=(vmem, vmem),
        scratch_shapes=[
            pltpu.VMEM((n, length, rows), BF16),
            pltpu.VMEM((n, length, 2 * E), BF16),
            pltpu.VMEM((n, E + 32, E), BF16),
            pltpu.VMEM((2, length, E), BF16),
            pltpu.VMEM((2, length, E), BF16),
            pltpu.VMEM((2, length, E), BF16),
            pltpu.VMEM((length, E), F32),
            pltpu.VMEM((length, E), F32),
            pltpu.VMEM((E, E), F32),
            dma((m,)),
            dma((n,)),
            dma((2 * n,)),
            dma((2 * n,)),
            dma((2 * n,)),
            dma((n,)),
            dma((n,)),
            dma((2,)),
            dma((2,)),
            dma((2,)),
            dma((2,)),
        ],
        compiler_params=pltpu.CompilerParams(
            collective_id=0, has_side_effects=True, vmem_limit_bytes=32 * 1024 * 1024
        ),
    )(layer_input, queries, keys, values, result_cotangent, log_decay)


def solution(mesh):
    in_specs = (
        P("ctx", "head"),
        P("ctx", "head"),
        P("ctx", "head"),
        P("ctx", "head"),
        P("ctx", "head"),
        P("head", "ctx"),
    )
    out_specs = (P("ctx", "head"), P("ctx", "head"))
    n, heads = mesh.shape["ctx"], mesh.shape["head"]

    def body(*args):
        return (fused if fits(args, n, heads) else on_device)(*args)

    return jax.shard_map(
        body, mesh=mesh, in_specs=in_specs, out_specs=out_specs, check_vma=False
    )
```

```python
import functools

import jax
import jax.numpy as jnp
from jax import lax
from jax.experimental import pallas as pl
from jax.experimental.pallas import tpu as pltpu
from jax.sharding import PartitionSpec as P

E = 128
WINDOW = 256


neg_fill = -1e30


def entering(array, axis, combine, identity):
    size, position = (lax.axis_size(axis), lax.axis_index(axis))
    everything = jax.tree.map(lambda part: lax.all_gather(part, axis), array)
    start = jax.tree.map(
        lambda part, zero: jnp.broadcast_to(jnp.asarray(zero, part.dtype), part.shape),
        array,
        identity,
    )

    def turn(k, before):
        at = size - 1 - k
        reached = at > position
        new = combine(before, jax.tree.map(lambda part: part[at], everything))
        return jax.tree.map(lambda a, b: jnp.where(reached, a, b), new, before)

    return lax.fori_loop(0, size, turn, start)


def shifted(value, axis, steps):
    count = lax.axis_size(axis)
    leading, last = (max(0, -steps), min(count, count - steps))
    return lax.ppermute(value, axis, [(source, source + steps) for source in range(leading, last)])


def band_grads(q_block, h_block, key_rows, value_rows, query_pos, key_pos):
    head_dim = key_rows.shape[1]
    group_size = q_block.shape[1] // head_dim
    row_count = q_block.shape[0]
    q_heads = q_block.reshape(row_count, group_size, head_dim)
    h_heads = h_block.reshape(row_count, group_size, head_dim)
    factor = head_dim ** (-0.5)
    scores = (
        jnp.einsum("trd,jd->rtj", q_heads, key_rows, preferred_element_type=jnp.float32) * factor
    )
    offset = query_pos[:, None] - key_pos[None, :]
    inside = (offset >= 0) & (offset < WINDOW) & (key_pos[None, :] >= 0)
    scores = jnp.where(inside[None], scores, neg_fill)
    row_max = jnp.max(scores, axis=2, keepdims=True)
    expo = jnp.exp(scores - row_max)
    attend = expo / jnp.sum(expo, axis=2, keepdims=True)
    attend_low = attend.astype(jnp.bfloat16)
    dprob = jnp.einsum("trd,jd->rtj", h_heads, value_rows, preferred_element_type=jnp.float32)
    row_delta = jnp.sum(attend * dprob, axis=2, keepdims=True)
    dscore = (attend * (dprob - row_delta)).astype(jnp.bfloat16)
    key_part = (
        jnp.einsum("rtj,trd->jd", dscore, q_heads, preferred_element_type=jnp.float32) * factor
    )
    value_part = jnp.einsum("rtj,trd->jd", attend_low, h_heads, preferred_element_type=jnp.float32)
    return (key_part, value_part)


def linear_terms(q_block, h_block, key_rows, value_rows, log_rates, lin_scale):
    head_dim = key_rows.shape[1]
    group_size = q_block.shape[1] // head_dim
    length = q_block.shape[0]
    q_heads = q_block.reshape(length, group_size, head_dim)
    h_heads = h_block.reshape(length, group_size, head_dim)
    row_after = lax.broadcasted_iota(jnp.int32, (length, length), 0)
    row_before = lax.broadcasted_iota(jnp.int32, (length, length), 1)
    log_sums = jnp.sum(jnp.where(row_after >= row_before, log_rates[None, :], 0.0), axis=1)
    mixing = jnp.exp(
        jnp.where(row_after >= row_before, log_sums[:, None] - log_sums[None, :], neg_fill)
    )
    key_mix = (
        mixing[None]
        * jnp.einsum("trd,jd->rtj", h_heads, value_rows, preferred_element_type=jnp.float32)
    ).astype(jnp.bfloat16)
    value_mix = (
        mixing[None]
        * jnp.einsum("trd,jd->rtj", q_heads, key_rows, preferred_element_type=jnp.float32)
    ).astype(jnp.bfloat16)
    key_part = (
        jnp.einsum("rtj,trd->jd", key_mix, q_heads, preferred_element_type=jnp.float32) * lin_scale
    )
    value_part = (
        jnp.einsum("rtj,trd->jd", value_mix, h_heads, preferred_element_type=jnp.float32)
        * lin_scale
    )
    weighted = (jnp.exp(log_sums)[:, None, None] * h_heads).astype(jnp.bfloat16)
    block_grad = (
        jnp.einsum("trd,tre->de", q_heads, weighted, preferred_element_type=jnp.float32) * lin_scale
    )
    return (
        key_part,
        value_part,
        block_grad,
        jnp.exp(log_sums[-1]),
        jnp.exp(log_sums[-1] - log_sums),
    )


def compose(earlier, later):
    return (later[0] * earlier[0], later[0][:, None, None] * earlier[1] + later[1])


def on_device(layer_input, queries, keys, values, result_cotangent, log_decay):
    length = queries.shape[0]
    head_dim = E
    lin_scale = 1.0 / (32 * head_dim)
    halves = result_cotangent * 0.5
    row_start = lax.axis_index("ctx") * length
    query_pos = row_start + jnp.arange(length, dtype=jnp.int32)
    key_pos = row_start - WINDOW + jnp.arange(length + WINDOW, dtype=jnp.int32)
    linear_parts = [linear_terms(queries, halves, keys, values, log_decay[0], lin_scale)]
    decays = jnp.stack([part[3] for part in linear_parts])
    block_grads = jnp.stack([part[2] for part in linear_parts])
    identity = (jnp.ones_like(decays), jnp.zeros_like(block_grads))
    _, incoming = entering((decays, block_grads), "ctx", compose, identity)
    preceding_keys, prior_v = shifted((keys, values), "ctx", 1)
    full_k = jnp.concatenate([preceding_keys, keys], axis=0)
    full_v = jnp.concatenate([prior_v, values], axis=0)
    band_parts = [band_grads(queries, halves, full_k, full_v, query_pos, key_pos)]
    win_k = jnp.concatenate([part[0] for part in band_parts], axis=1)
    win_v = jnp.concatenate([part[1] for part in band_parts], axis=1)
    back_k, back_v = shifted((win_k[:WINDOW], win_v[:WINDOW]), "ctx", -1)
    win_k = win_k[WINDOW:]
    win_v = win_v[WINDOW:]
    zero_rows = jnp.zeros((length - WINDOW, win_k.shape[1]), jnp.float32)
    win_k = win_k + jnp.concatenate([zero_rows, back_k], axis=0)
    win_v = win_v + jnp.concatenate([zero_rows, back_v], axis=0)
    state_in = incoming[0]
    tail_decay = linear_parts[0][4][:, None]
    lin_keys = linear_parts[0][0] + tail_decay * jnp.dot(
        values.astype(jnp.float32), state_in.T, precision=lax.Precision.HIGHEST
    )
    lin_values = linear_parts[0][1] + tail_decay * jnp.dot(
        keys.astype(jnp.float32), state_in, precision=lax.Precision.HIGHEST
    )
    key_grad = (lin_keys + win_k).astype(jnp.bfloat16)
    value_grad = (lin_values + win_v).astype(jnp.bfloat16)
    both_grads = jnp.concatenate([key_grad, value_grad], axis=1)
    partial_value = lax.dot_general(
        lax.all_gather(layer_input, "head", axis=1, tiled=True),
        both_grads,
        (((0,), (0,)), ((), ())),
        preferred_element_type=jnp.float32,
    )
    owned = lax.psum_scatter(partial_value, "ctx", scatter_dimension=0, tiled=True)
    key_width = key_grad.shape[1]
    return (owned[:, :key_width].astype(jnp.bfloat16), owned[:, key_width:].astype(jnp.bfloat16))


MESH = pl.DeviceIdType.MESH
F32, BF16 = jnp.float32, jnp.bfloat16


def fits(args, n, heads):
    x, q, k = args[0], args[1], args[2]
    rows = x.shape[1] * heads // n
    return (
        heads == 4
        and n == 2 * heads
        and rows % 128 == 0
        and x.shape[0] == WINDOW
        and k.shape[1] == E
        and q.shape[1] % E == 0
        and x.shape[1] == 2 * rows
    )


def tn(a, b):
    return lax.dot_general(a, b, (((0,), (0,)), ((), ())), preferred_element_type=F32)


def nt(a, b):
    return lax.dot_general(a, b, (((1,), (1,)), ((), ())), preferred_element_type=F32)


def fused_kernel(
    n, m, x_ref, q_hbm, k_hbm, v_hbm, d_hbm, ld_hbm, ok_ref, ov_ref,
    q_ref, k_ref, v_ref, d_ref, ld_ref, in_sem, xall, gall, sall, halo, back_out, back_in, part_k, part_v, state,
    x_send, x_recv, x_own, f_send, g_up, g_down, g_side, g_recv, s_send, s_recv, h_send, h_recv, b_send, b_recv,
):
    length, width = q_ref.shape
    group = width // E
    rows = x_ref.shape[1] // m
    part = length // 2
    factor = E ** (-0.5)
    lin_scale = 1.0 / (32 * E)
    c, h = lax.axis_index("ctx"), lax.axis_index("head")
    owner = c // m
    sibling = h + 1 - 2 * lax.rem(h, 2)
    across = lax.rem(h + 2, 4)

    def copy(src, dst, send, recv, ctx, head):
        return pltpu.make_async_remote_copy(
            src_ref=src, dst_ref=dst, send_sem=send, recv_sem=recv,
            device_id=(ctx, head), device_id_type=MESH,
        )

    loads = [
        pltpu.make_async_copy(src, dst, in_sem.at[i])
        for i, (src, dst) in enumerate(
            ((ld_hbm, ld_ref), (q_hbm, q_ref), (d_hbm, d_ref), (k_hbm, k_ref), (v_hbm, v_ref))
        )
    ]
    for load in loads:
        load.start()

    peers = [lax.rem(c + i, n) for i in range(1, n)]
    barrier = pltpu.get_barrier_semaphore()
    for p in peers:
        pl.semaphore_signal(barrier, inc=1, device_id=(p, h), device_id_type=MESH)
        pl.semaphore_signal(barrier, inc=1, device_id=(p, across), device_id_type=MESH)
    for i in range(1, 4):
        pl.semaphore_signal(
            barrier, inc=1, device_id=(c, lax.rem(h + i, 4)), device_id_type=MESH
        )
    pl.semaphore_wait(barrier, 2 * n + 1)

    def halo_copy(i):
        return copy(
            (k_hbm, v_hbm)[i], halo.at[i], h_send.at[i], h_recv.at[i], lax.rem(c + 1, n), h
        )

    @pl.when(c < n - 1)
    def _():
        halo_copy(0).start()
        halo_copy(1).start()

    @pl.when(c == 0)
    def _():
        halo[...] = jnp.zeros_like(halo)

    def x_copy(j, p):
        return copy(
            x_ref.at[pl.ds(p * part, part), pl.ds(j * rows, rows)], xall.at[p, c],
            x_send.at[j, p], x_recv.at[p, c], h * m + j, (h, across)[p],
        )

    def x_local(j):
        return pltpu.make_async_copy(
            x_ref.at[pl.ds(0, part), pl.ds(j * rows, rows)], xall.at[0, c], x_own
        )

    for j in range(m):

        @pl.when(h * m + j == c)
        def _():
            x_local(j).start()

        @pl.when(h * m + j != c)
        def _():
            x_copy(j, 0).start()

        x_copy(j, 1).start()

    for load in loads:
        load.wait()

    after = lax.broadcasted_iota(jnp.int32, (length, length), 0)
    before = lax.broadcasted_iota(jnp.int32, (length, length), 1)
    lower = after >= before
    sums = jnp.sum(jnp.where(lower, ld_ref[...], 0.0), axis=1, keepdims=True)
    sums_row = jnp.sum(jnp.where(after == before, sums, 0.0), axis=0, keepdims=True)
    total = jnp.sum(ld_ref[...], axis=1, keepdims=True)

    grown = jnp.exp(sums)
    qs, hs, grad = [], [], jnp.zeros((E, E), F32)
    for r in range(group):
        qs.append(q_ref[:, r * E : (r + 1) * E])
        hs.append((d_ref[:, r * E : (r + 1) * E].astype(F32) * 0.5).astype(BF16))
        grad += tn(qs[r], (grown * hs[r].astype(F32)).astype(BF16))
    decay = jnp.broadcast_to(jnp.exp(total), (16, E))
    coarse = decay.astype(BF16)
    fine = (decay - coarse.astype(F32)).astype(BF16)
    sall[c, 0:E, :] = (grad * lin_scale).astype(BF16)
    sall[c, E : E + 16, :] = coarse
    sall[c, E + 16 : E + 32, :] = fine

    def state_copy(i):
        return copy(
            sall.at[c], sall.at[c], s_send.at[i], s_recv.at[c], lax.rem(c + n - i, n), h
        )

    for i in range(1, n):

        @pl.when(c - i >= 0)
        def _():
            state_copy(i).start()

    mixing = jnp.exp(jnp.where(lower, sums - sums_row, neg_fill))
    keys, vals = k_ref[...], v_ref[...]
    lin_k = jnp.zeros((length, E), F32)
    lin_v = jnp.zeros((length, E), F32)
    own_s, own_p = [], []
    for r in range(group):
        own_s.append(nt(qs[r], keys))
        own_p.append(nt(hs[r], vals))
        lin_k += tn((mixing * own_p[r]).astype(BF16), qs[r])
        lin_v += tn((mixing * own_s[r]).astype(BF16), hs[r])

    @pl.when(c > 0)
    def _():
        halo_copy(0).wait_recv()
        halo_copy(1).wait_recv()

    old_k, old_v = halo[0], halo[1]
    upper = jnp.logical_and(before > after, c > 0)
    win = [jnp.zeros((length, E), F32) for _ in range(4)]
    for r in range(group):
        s_own = jnp.where(lower, own_s[r] * factor, neg_fill)
        s_old = jnp.where(upper, nt(qs[r], old_k) * factor, neg_fill)
        top = jnp.maximum(
            jnp.max(s_own, axis=1, keepdims=True), jnp.max(s_old, axis=1, keepdims=True)
        )
        e_own, e_old = jnp.exp(s_own - top), jnp.exp(s_old - top)
        inv = 1.0 / (jnp.sum(e_own, axis=1, keepdims=True) + jnp.sum(e_old, axis=1, keepdims=True))
        a_own, a_old = e_own * inv, e_old * inv
        p_old = nt(hs[r], old_v)
        delta = jnp.sum(a_own * own_p[r], axis=1, keepdims=True) + jnp.sum(
            a_old * p_old, axis=1, keepdims=True
        )
        win[0] += tn((a_old * (p_old - delta)).astype(BF16), qs[r])
        win[1] += tn(a_old.astype(BF16), hs[r])
        win[2] += tn((a_own * (own_p[r] - delta)).astype(BF16), qs[r])
        win[3] += tn(a_own.astype(BF16), hs[r])
    back_out[0] = (win[0] * factor).astype(BF16)
    back_out[1] = win[1].astype(BF16)

    def back_copy(i):
        return copy(
            back_out.at[i], back_in.at[i], b_send.at[i], b_recv.at[i], lax.rem(c + n - 1, n), h
        )

    @pl.when(c > 0)
    def _():
        back_copy(0).start()
        back_copy(1).start()

    part_k[...] = lin_k * lin_scale + win[2] * factor
    part_v[...] = lin_v * lin_scale + win[3]

    def forward(p, slot, i, head):
        return copy(xall.at[p, slot], xall.at[p, slot], f_send.at[i], x_recv.at[p, slot], c, head)

    def arrived(p, slot):
        return copy(
            xall.at[p, slot], xall.at[p, slot], x_send.at[0, 0], x_recv.at[p, slot], c, sibling
        )

    roots = (h == owner, across == owner)
    for p in range(2):

        @pl.when(roots[p])
        def _():
            for i in range(n - 1, -1, -1):
                slot = lax.rem(c + i, n)
                if i or p:
                    arrived(p, slot).wait_recv()
                else:
                    x_local(0).wait()
                forward(p, slot, 3 * i, across).start()
                forward(p, slot, 3 * i + 1, sibling).start()

    state[...] = jnp.zeros_like(state)
    for i in range(n - 1, 0, -1):

        @pl.when(c + i < n)
        def _():
            slot = lax.rem(c + i, n)
            copy(
                sall.at[slot], sall.at[slot], s_send.at[0], s_recv.at[slot], slot, h
            ).wait_recv()
            kept = sall[slot, E : E + 1, :].astype(F32) + sall[slot, E + 16 : E + 17, :].astype(F32)
            state[...] = kept * state[...] + sall[slot, 0:E, :].astype(F32)

    high = state[...].astype(BF16)
    low = (state[...] - high.astype(F32)).astype(BF16)
    ending = jnp.exp(total - sums)
    part_k[...] += ending * (nt(vals, high) + nt(vals, low))
    part_v[...] += ending * (
        jnp.dot(keys, high, preferred_element_type=F32)
        + jnp.dot(keys, low, preferred_element_type=F32)
    )

    @pl.when(c < n - 1)
    def _():
        back_copy(0).wait_recv()
        back_copy(1).wait_recv()
        part_k[...] += back_in[0].astype(F32)
        part_v[...] += back_in[1].astype(F32)

    gall[0, c] = part_k[...].astype(BF16)
    gall[1, c] = part_v[...].astype(BF16)

    side = c + 1 - 2 * lax.rem(c, 2)
    up_ok, down_ok = c < n - 2, c >= 2

    def up(p, slot):
        return copy(gall.at[p, slot], gall.at[p, slot], g_up.at[p, slot], g_recv.at[p, slot], lax.rem(c + 2, n), h)

    def down(p, slot):
        return copy(gall.at[p, slot], gall.at[p, slot], g_down.at[p, slot], g_recv.at[p, slot], lax.rem(c + n - 2, n), h)

    def beside(p, slot):
        return copy(gall.at[p, slot], gall.at[p, slot], g_side.at[p, slot], g_recv.at[p, slot], side, h)

    def along(act, p, slot, upward, downward):
        if upward:

            @pl.when(up_ok)
            def _():
                act(up(p, slot))

        if downward:

            @pl.when(down_ok)
            def _():
                act(down(p, slot))

    def start(dma):
        dma.start()

    def sent(dma):
        dma.wait_send()

    def arrive(p, slot):
        beside(p, slot).wait_recv()

    def spread(act, wait):
        act(beside(0, c))
        along(act, 0, c, True, True)
        along(act, 1, c, True, True)
        act(beside(1, c))
        if wait:
            arrive(0, side)
        along(act, 0, side, True, True)
        for d in range(2, n, 2):

            @pl.when(c - d >= 0)
            def _():
                for p, slot in ((0, c - d), (1, c - d), (0, side - d)):
                    if wait:
                        arrive(p, slot)
                    along(act, p, slot, True, False)
                    if p:
                        act(beside(p, slot))

            @pl.when(c + d < n)
            def _():
                for p, slot in ((0, c + d), (1, c + d), (0, side + d)):
                    if wait:
                        arrive(p, slot)
                    along(act, p, slot, False, True)
                    if p:
                        act(beside(p, slot))

    spread(start, True)

    for p in range(2):

        @pl.when(roots[1 - p])
        def _():
            for i in range(n - 1, -1, -1):
                slot = lax.rem(c + i, n)
                arrived(p, slot).wait_recv()
                forward(p, slot, 3 * i + 2, sibling).start()

    @pl.when(lax.rem(h + owner, 2) == 1)
    def _():
        for slot in range(n):
            arrived(0, slot).wait_recv()
            arrived(1, slot).wait_recv()

    for i in range(0, n, 2):
        slot = lax.rem(side + i, n)
        arrive(1, slot)
    acc_k = jnp.zeros((rows, E), F32)
    acc_v = jnp.zeros((rows, E), F32)
    for slot in range(n):
        both = xall[:, slot].reshape(length, rows)
        acc_k += tn(both, gall[0, slot])
        acc_v += tn(both, gall[1, slot])
    ok_ref[...] = acc_k.astype(BF16)
    ov_ref[...] = acc_v.astype(BF16)

    @pl.when(c < n - 1)
    def _():
        halo_copy(0).wait_send()
        halo_copy(1).wait_send()

    @pl.when(c > 0)
    def _():
        back_copy(0).wait_send()
        back_copy(1).wait_send()

    for j in range(m):

        @pl.when(h * m + j != c)
        def _():
            x_copy(j, 0).wait_send()

        x_copy(j, 1).wait_send()

    for i in range(1, n):

        @pl.when(c - i >= 0)
        def _():
            state_copy(i).wait_send()

    for p in range(2):

        @pl.when(roots[p])
        def _():
            for i in range(n):
                slot = lax.rem(c + i, n)
                forward(p, slot, 3 * i, across).wait_send()
                forward(p, slot, 3 * i + 1, sibling).wait_send()
                forward(1 - p, slot, 3 * i + 2, sibling).wait_send()

    spread(sent, False)


def fused(layer_input, queries, keys, values, result_cotangent, log_decay):
    n = lax.axis_size("ctx")
    length, width = layer_input.shape
    rows = width * lax.axis_size("head") // n
    m = width // rows
    dma = pltpu.SemaphoreType.DMA
    shape = jax.ShapeDtypeStruct((rows, E), BF16)
    vmem = pl.BlockSpec(memory_space=pltpu.VMEM)
    return pl.pallas_call(
        functools.partial(fused_kernel, n, m),
        out_shape=(shape, shape),
        in_specs=[pl.BlockSpec(memory_space=pltpu.HBM)] * 6,
        out_specs=(vmem, vmem),
        scratch_shapes=[
            pltpu.VMEM(queries.shape, BF16),
            pltpu.VMEM(keys.shape, BF16),
            pltpu.VMEM(values.shape, BF16),
            pltpu.VMEM(queries.shape, BF16),
            pltpu.VMEM(log_decay.shape, F32),
            dma((5,)),
            pltpu.VMEM((2, n, length // 2, rows), BF16),
            pltpu.VMEM((2, n, length, E), BF16),
            pltpu.VMEM((n, E + 32, E), BF16),
            pltpu.VMEM((2, length, E), BF16),
            pltpu.VMEM((2, length, E), BF16),
            pltpu.VMEM((2, length, E), BF16),
            pltpu.VMEM((length, E), F32),
            pltpu.VMEM((length, E), F32),
            pltpu.VMEM((E, E), F32),
            dma((m, 2)),
            dma((2, n)),
            dma,
            dma((3 * n,)),
            dma((2, n)),
            dma((2, n)),
            dma((2, n)),
            dma((2, n)),
            dma((n,)),
            dma((n,)),
            dma((2,)),
            dma((2,)),
            dma((2,)),
            dma((2,)),
        ],
        compiler_params=pltpu.CompilerParams(
            collective_id=0, has_side_effects=True, vmem_limit_bytes=32 * 1024 * 1024
        ),
    )(layer_input, queries, keys, values, result_cotangent, log_decay)


def solution(mesh):
    in_specs = (
        P("ctx", "head"),
        P("ctx", "head"),
        P("ctx", "head"),
        P("ctx", "head"),
        P("ctx", "head"),
        P("head", "ctx"),
    )
    out_specs = (P("ctx", "head"), P("ctx", "head"))
    n, heads = mesh.shape["ctx"], mesh.shape["head"]

    def body(*args):
        return (fused if fits(args, n, heads) else on_device)(*args)

    return jax.shard_map(
        body, mesh=mesh, in_specs=in_specs, out_specs=out_specs, check_vma=False
    )
```

```python
import functools

import jax
import jax.numpy as jnp
from jax import lax
from jax.experimental import pallas as pl
from jax.experimental.pallas import tpu as pltpu
from jax.sharding import PartitionSpec as P

E = 128
WINDOW = 256


neg_fill = -1e30


def entering(array, axis, combine, identity):
    size, position = (lax.axis_size(axis), lax.axis_index(axis))
    everything = jax.tree.map(lambda part: lax.all_gather(part, axis), array)
    start = jax.tree.map(
        lambda part, zero: jnp.broadcast_to(jnp.asarray(zero, part.dtype), part.shape),
        array,
        identity,
    )

    def turn(k, before):
        at = size - 1 - k
        reached = at > position
        new = combine(before, jax.tree.map(lambda part: part[at], everything))
        return jax.tree.map(lambda a, b: jnp.where(reached, a, b), new, before)

    return lax.fori_loop(0, size, turn, start)


def shifted(value, axis, steps):
    count = lax.axis_size(axis)
    leading, last = (max(0, -steps), min(count, count - steps))
    return lax.ppermute(value, axis, [(source, source + steps) for source in range(leading, last)])


def band_grads(q_block, h_block, key_rows, value_rows, query_pos, key_pos):
    head_dim = key_rows.shape[1]
    group_size = q_block.shape[1] // head_dim
    row_count = q_block.shape[0]
    q_heads = q_block.reshape(row_count, group_size, head_dim)
    h_heads = h_block.reshape(row_count, group_size, head_dim)
    factor = head_dim ** (-0.5)
    scores = (
        jnp.einsum("trd,jd->rtj", q_heads, key_rows, preferred_element_type=jnp.float32) * factor
    )
    offset = query_pos[:, None] - key_pos[None, :]
    inside = (offset >= 0) & (offset < WINDOW) & (key_pos[None, :] >= 0)
    scores = jnp.where(inside[None], scores, neg_fill)
    row_max = jnp.max(scores, axis=2, keepdims=True)
    expo = jnp.exp(scores - row_max)
    attend = expo / jnp.sum(expo, axis=2, keepdims=True)
    attend_low = attend.astype(jnp.bfloat16)
    dprob = jnp.einsum("trd,jd->rtj", h_heads, value_rows, preferred_element_type=jnp.float32)
    row_delta = jnp.sum(attend * dprob, axis=2, keepdims=True)
    dscore = (attend * (dprob - row_delta)).astype(jnp.bfloat16)
    key_part = (
        jnp.einsum("rtj,trd->jd", dscore, q_heads, preferred_element_type=jnp.float32) * factor
    )
    value_part = jnp.einsum("rtj,trd->jd", attend_low, h_heads, preferred_element_type=jnp.float32)
    return (key_part, value_part)


def linear_terms(q_block, h_block, key_rows, value_rows, log_rates, lin_scale):
    head_dim = key_rows.shape[1]
    group_size = q_block.shape[1] // head_dim
    length = q_block.shape[0]
    q_heads = q_block.reshape(length, group_size, head_dim)
    h_heads = h_block.reshape(length, group_size, head_dim)
    row_after = lax.broadcasted_iota(jnp.int32, (length, length), 0)
    row_before = lax.broadcasted_iota(jnp.int32, (length, length), 1)
    log_sums = jnp.sum(jnp.where(row_after >= row_before, log_rates[None, :], 0.0), axis=1)
    mixing = jnp.exp(
        jnp.where(row_after >= row_before, log_sums[:, None] - log_sums[None, :], neg_fill)
    )
    key_mix = (
        mixing[None]
        * jnp.einsum("trd,jd->rtj", h_heads, value_rows, preferred_element_type=jnp.float32)
    ).astype(jnp.bfloat16)
    value_mix = (
        mixing[None]
        * jnp.einsum("trd,jd->rtj", q_heads, key_rows, preferred_element_type=jnp.float32)
    ).astype(jnp.bfloat16)
    key_part = (
        jnp.einsum("rtj,trd->jd", key_mix, q_heads, preferred_element_type=jnp.float32) * lin_scale
    )
    value_part = (
        jnp.einsum("rtj,trd->jd", value_mix, h_heads, preferred_element_type=jnp.float32)
        * lin_scale
    )
    weighted = (jnp.exp(log_sums)[:, None, None] * h_heads).astype(jnp.bfloat16)
    block_grad = (
        jnp.einsum("trd,tre->de", q_heads, weighted, preferred_element_type=jnp.float32) * lin_scale
    )
    return (
        key_part,
        value_part,
        block_grad,
        jnp.exp(log_sums[-1]),
        jnp.exp(log_sums[-1] - log_sums),
    )


def compose(earlier, later):
    return (later[0] * earlier[0], later[0][:, None, None] * earlier[1] + later[1])


def on_device(layer_input, queries, keys, values, result_cotangent, log_decay):
    length = queries.shape[0]
    head_dim = E
    lin_scale = 1.0 / (32 * head_dim)
    halves = result_cotangent * 0.5
    row_start = lax.axis_index("ctx") * length
    query_pos = row_start + jnp.arange(length, dtype=jnp.int32)
    key_pos = row_start - WINDOW + jnp.arange(length + WINDOW, dtype=jnp.int32)
    linear_parts = [linear_terms(queries, halves, keys, values, log_decay[0], lin_scale)]
    decays = jnp.stack([part[3] for part in linear_parts])
    block_grads = jnp.stack([part[2] for part in linear_parts])
    identity = (jnp.ones_like(decays), jnp.zeros_like(block_grads))
    _, incoming = entering((decays, block_grads), "ctx", compose, identity)
    preceding_keys, prior_v = shifted((keys, values), "ctx", 1)
    full_k = jnp.concatenate([preceding_keys, keys], axis=0)
    full_v = jnp.concatenate([prior_v, values], axis=0)
    band_parts = [band_grads(queries, halves, full_k, full_v, query_pos, key_pos)]
    win_k = jnp.concatenate([part[0] for part in band_parts], axis=1)
    win_v = jnp.concatenate([part[1] for part in band_parts], axis=1)
    back_k, back_v = shifted((win_k[:WINDOW], win_v[:WINDOW]), "ctx", -1)
    win_k = win_k[WINDOW:]
    win_v = win_v[WINDOW:]
    zero_rows = jnp.zeros((length - WINDOW, win_k.shape[1]), jnp.float32)
    win_k = win_k + jnp.concatenate([zero_rows, back_k], axis=0)
    win_v = win_v + jnp.concatenate([zero_rows, back_v], axis=0)
    state_in = incoming[0]
    tail_decay = linear_parts[0][4][:, None]
    lin_keys = linear_parts[0][0] + tail_decay * jnp.dot(
        values.astype(jnp.float32), state_in.T, precision=lax.Precision.HIGHEST
    )
    lin_values = linear_parts[0][1] + tail_decay * jnp.dot(
        keys.astype(jnp.float32), state_in, precision=lax.Precision.HIGHEST
    )
    key_grad = (lin_keys + win_k).astype(jnp.bfloat16)
    value_grad = (lin_values + win_v).astype(jnp.bfloat16)
    both_grads = jnp.concatenate([key_grad, value_grad], axis=1)
    partial_value = lax.dot_general(
        lax.all_gather(layer_input, "head", axis=1, tiled=True),
        both_grads,
        (((0,), (0,)), ((), ())),
        preferred_element_type=jnp.float32,
    )
    owned = lax.psum_scatter(partial_value, "ctx", scatter_dimension=0, tiled=True)
    key_width = key_grad.shape[1]
    return (owned[:, :key_width].astype(jnp.bfloat16), owned[:, key_width:].astype(jnp.bfloat16))


MESH = pl.DeviceIdType.MESH
F32, BF16 = jnp.float32, jnp.bfloat16


def fits(args, n, heads):
    x, q, k = args[0], args[1], args[2]
    rows = x.shape[1] * heads // n
    return (
        heads == 4
        and n == 2 * heads
        and rows % 128 == 0
        and x.shape[0] == WINDOW
        and k.shape[1] == E
        and q.shape[1] % E == 0
        and x.shape[1] == 2 * rows
    )


def tn(a, b):
    return lax.dot_general(a, b, (((0,), (0,)), ((), ())), preferred_element_type=F32)


def nt(a, b):
    return lax.dot_general(a, b, (((1,), (1,)), ((), ())), preferred_element_type=F32)


def fused_kernel(
    n, m, x_ref, q_hbm, k_hbm, v_hbm, d_hbm, ld_hbm, ok_ref, ov_ref,
    q_ref, k_ref, v_ref, d_ref, ld_ref, in_sem, xall, gall, sall, halo, back_out, back_in, part_k, part_v, state, chain_out, chain_in,
    x_send, x_recv, x_own, f_send, g_up, g_down, g_side, g_recv, s_send, s_recv, h_send, h_recv, b_send, b_recv,
):
    length, width = q_ref.shape
    group = width // E
    rows = x_ref.shape[1] // m
    part = length // 2
    factor = E ** (-0.5)
    lin_scale = 1.0 / (32 * E)
    c, h = lax.axis_index("ctx"), lax.axis_index("head")
    owner = c // m
    sibling = h + 1 - 2 * lax.rem(h, 2)
    across = lax.rem(h + 2, 4)

    def copy(src, dst, send, recv, ctx, head):
        return pltpu.make_async_remote_copy(
            src_ref=src, dst_ref=dst, send_sem=send, recv_sem=recv,
            device_id=(ctx, head), device_id_type=MESH,
        )

    loads = [
        pltpu.make_async_copy(src, dst, in_sem.at[i])
        for i, (src, dst) in enumerate(
            ((ld_hbm, ld_ref), (q_hbm, q_ref), (d_hbm, d_ref), (k_hbm, k_ref), (v_hbm, v_ref))
        )
    ]
    for load in loads:
        load.start()

    peers = [lax.rem(c + i, n) for i in range(1, n)]
    barrier = pltpu.get_barrier_semaphore()
    for p in peers:
        pl.semaphore_signal(barrier, inc=1, device_id=(p, h), device_id_type=MESH)
        pl.semaphore_signal(barrier, inc=1, device_id=(p, across), device_id_type=MESH)
    for i in range(1, 4):
        pl.semaphore_signal(
            barrier, inc=1, device_id=(c, lax.rem(h + i, 4)), device_id_type=MESH
        )
    pl.semaphore_wait(barrier, 2 * n + 1)

    def halo_copy(i):
        return copy(
            (k_hbm, v_hbm)[i], halo.at[i], h_send.at[i], h_recv.at[i], lax.rem(c + 1, n), h
        )

    @pl.when(c < n - 1)
    def _():
        halo_copy(0).start()
        halo_copy(1).start()

    @pl.when(c == 0)
    def _():
        halo[...] = jnp.zeros_like(halo)

    def x_copy(j, p):
        return copy(
            x_ref.at[pl.ds(p * part, part), pl.ds(j * rows, rows)], xall.at[p, c],
            x_send.at[j, p], x_recv.at[p, c], h * m + j, (h, across)[p],
        )

    def x_local(j):
        return pltpu.make_async_copy(
            x_ref.at[pl.ds(0, part), pl.ds(j * rows, rows)], xall.at[0, c], x_own
        )

    for j in range(m):

        @pl.when(h * m + j == c)
        def _():
            x_local(j).start()

        @pl.when(h * m + j != c)
        def _():
            x_copy(j, 0).start()

        x_copy(j, 1).start()

    for load in loads:
        load.wait()

    after = lax.broadcasted_iota(jnp.int32, (length, length), 0)
    before = lax.broadcasted_iota(jnp.int32, (length, length), 1)
    lower = after >= before
    sums = jnp.sum(jnp.where(lower, ld_ref[...], 0.0), axis=1, keepdims=True)
    sums_row = jnp.sum(jnp.where(after == before, sums, 0.0), axis=0, keepdims=True)
    total = jnp.sum(ld_ref[...], axis=1, keepdims=True)

    grown = jnp.exp(sums)
    qs, hs, grad = [], [], jnp.zeros((E, E), F32)
    for r in range(group):
        qs.append(q_ref[:, r * E : (r + 1) * E])
        hs.append((d_ref[:, r * E : (r + 1) * E].astype(F32) * 0.5).astype(BF16))
        grad += tn(qs[r], (grown * hs[r].astype(F32)).astype(BF16))
    decay = jnp.broadcast_to(jnp.exp(total), (16, E))
    coarse = decay.astype(BF16)
    fine = (decay - coarse.astype(F32)).astype(BF16)
    sall[c, 0:E, :] = (grad * lin_scale).astype(BF16)
    sall[c, E : E + 16, :] = coarse
    sall[c, E + 16 : E + 32, :] = fine

    side = c + 1 - 2 * lax.rem(c, 2)

    def state_copy():
        return copy(sall.at[c], sall.at[c], s_send.at[0], s_recv.at[c], side, h)

    state_copy().start()

    mixing = jnp.exp(jnp.where(lower, sums - sums_row, neg_fill))
    keys, vals = k_ref[...], v_ref[...]
    lin_k = jnp.zeros((length, E), F32)
    lin_v = jnp.zeros((length, E), F32)
    own_s, own_p = [], []
    for r in range(group):
        own_s.append(nt(qs[r], keys))
        own_p.append(nt(hs[r], vals))
        lin_k += tn((mixing * own_p[r]).astype(BF16), qs[r])
        lin_v += tn((mixing * own_s[r]).astype(BF16), hs[r])

    @pl.when(c > 0)
    def _():
        halo_copy(0).wait_recv()
        halo_copy(1).wait_recv()

    old_k, old_v = halo[0], halo[1]
    upper = jnp.logical_and(before > after, c > 0)
    win = [jnp.zeros((length, E), F32) for _ in range(4)]
    for r in range(group):
        s_own = jnp.where(lower, own_s[r] * factor, neg_fill)
        s_old = jnp.where(upper, nt(qs[r], old_k) * factor, neg_fill)
        top = jnp.maximum(
            jnp.max(s_own, axis=1, keepdims=True), jnp.max(s_old, axis=1, keepdims=True)
        )
        e_own, e_old = jnp.exp(s_own - top), jnp.exp(s_old - top)
        inv = 1.0 / (jnp.sum(e_own, axis=1, keepdims=True) + jnp.sum(e_old, axis=1, keepdims=True))
        a_own, a_old = e_own * inv, e_old * inv
        p_old = nt(hs[r], old_v)
        delta = jnp.sum(a_own * own_p[r], axis=1, keepdims=True) + jnp.sum(
            a_old * p_old, axis=1, keepdims=True
        )
        win[0] += tn((a_old * (p_old - delta)).astype(BF16), qs[r])
        win[1] += tn(a_old.astype(BF16), hs[r])
        win[2] += tn((a_own * (own_p[r] - delta)).astype(BF16), qs[r])
        win[3] += tn(a_own.astype(BF16), hs[r])
    back_out[0] = (win[0] * factor).astype(BF16)
    back_out[1] = win[1].astype(BF16)

    def back_copy(i):
        return copy(
            back_out.at[i], back_in.at[i], b_send.at[i], b_recv.at[i], lax.rem(c + n - 1, n), h
        )

    @pl.when(c > 0)
    def _():
        back_copy(0).start()
        back_copy(1).start()

    part_k[...] = lin_k * lin_scale + win[2] * factor
    part_v[...] = lin_v * lin_scale + win[3]

    def forward(p, slot, i, head):
        return copy(xall.at[p, slot], xall.at[p, slot], f_send.at[i], x_recv.at[p, slot], c, head)

    def arrived(p, slot):
        return copy(
            xall.at[p, slot], xall.at[p, slot], x_send.at[0, 0], x_recv.at[p, slot], c, sibling
        )

    roots = (h == owner, across == owner)
    def chain():
        return copy(chain_out, chain_in, s_send.at[1], s_recv.at[n], lax.rem(c + n - 2, n), h)

    copy(sall.at[side], sall.at[side], s_send.at[0], s_recv.at[side], side, h).wait_recv()

    @pl.when(c >= n - 2)
    def _():
        chain_in[...] = jnp.zeros_like(chain_in)

    @pl.when(c < n - 2)
    def _():
        chain().wait_recv()

    def through(slot, later):
        kept = sall[slot, E : E + 1, :].astype(F32) + sall[slot, E + 16 : E + 17, :].astype(F32)
        return kept * later + sall[slot, 0:E, :].astype(F32)

    first = c - lax.rem(c, 2)
    beyond = chain_in[...]
    between = through(first + 1, beyond)

    @pl.when(c >= 2)
    def _():
        chain_out[...] = through(first, between)
        chain().start()

    state[...] = jnp.where(c == first, between, beyond)

    high = state[...].astype(BF16)
    low = (state[...] - high.astype(F32)).astype(BF16)
    ending = jnp.exp(total - sums)
    part_k[...] += ending * (nt(vals, high) + nt(vals, low))
    part_v[...] += ending * (
        jnp.dot(keys, high, preferred_element_type=F32)
        + jnp.dot(keys, low, preferred_element_type=F32)
    )

    @pl.when(c < n - 1)
    def _():
        back_copy(0).wait_recv()
        back_copy(1).wait_recv()
        part_k[...] += back_in[0].astype(F32)
        part_v[...] += back_in[1].astype(F32)

    gall[0, c] = part_k[...].astype(BF16)
    gall[1, c] = part_v[...].astype(BF16)

    up_ok, down_ok = c < n - 2, c >= 2

    def up(p, slot):
        return copy(gall.at[p, slot], gall.at[p, slot], g_up.at[p, slot], g_recv.at[p, slot], lax.rem(c + 2, n), h)

    def down(p, slot):
        return copy(gall.at[p, slot], gall.at[p, slot], g_down.at[p, slot], g_recv.at[p, slot], lax.rem(c + n - 2, n), h)

    def beside(p, slot):
        return copy(gall.at[p, slot], gall.at[p, slot], g_side.at[p, slot], g_recv.at[p, slot], side, h)

    def along(act, p, slot, upward, downward):
        if upward:

            @pl.when(up_ok)
            def _():
                act(up(p, slot))

        if downward:

            @pl.when(down_ok)
            def _():
                act(down(p, slot))

    def start(dma):
        dma.start()

    def sent(dma):
        dma.wait_send()

    def arrive(p, slot):
        beside(p, slot).wait_recv()

    def share(act):
        act(beside(0, c))
        along(act, 0, c, True, True)
        along(act, 1, c, True, True)
        act(beside(1, c))

    def spread(act, wait):
        if wait:
            arrive(0, side)
        along(act, 0, side, True, True)
        for d in range(2, n, 2):

            @pl.when(c - d >= 0)
            def _():
                for p, slot in ((0, c - d), (1, c - d), (0, side - d)):
                    if wait:
                        arrive(p, slot)
                    along(act, p, slot, True, False)
                    if p:
                        act(beside(p, slot))

            @pl.when(c + d < n)
            def _():
                for p, slot in ((0, c + d), (1, c + d), (0, side + d)):
                    if wait:
                        arrive(p, slot)
                    along(act, p, slot, False, True)
                    if p:
                        act(beside(p, slot))

    share(start)

    for p in range(2):

        @pl.when(roots[p])
        def _():
            for i in range(n - 1, -1, -1):
                slot = lax.rem(c + i, n)
                if i or p:
                    arrived(p, slot).wait_recv()
                else:
                    x_local(0).wait()
                forward(p, slot, 3 * i, across).start()
                forward(p, slot, 3 * i + 1, sibling).start()

    spread(start, True)

    for p in range(2):

        @pl.when(roots[1 - p])
        def _():
            for i in range(n - 1, -1, -1):
                slot = lax.rem(c + i, n)
                arrived(p, slot).wait_recv()
                forward(p, slot, 3 * i + 2, sibling).start()

    @pl.when(lax.rem(h + owner, 2) == 1)
    def _():
        for slot in range(n):
            arrived(0, slot).wait_recv()
            arrived(1, slot).wait_recv()

    for i in range(0, n, 2):
        slot = lax.rem(side + i, n)
        arrive(1, slot)
    acc_k = jnp.zeros((rows, E), F32)
    acc_v = jnp.zeros((rows, E), F32)
    for slot in range(n):
        both = xall[:, slot].reshape(length, rows)
        acc_k += tn(both, gall[0, slot])
        acc_v += tn(both, gall[1, slot])
    ok_ref[...] = acc_k.astype(BF16)
    ov_ref[...] = acc_v.astype(BF16)

    @pl.when(c < n - 1)
    def _():
        halo_copy(0).wait_send()
        halo_copy(1).wait_send()

    @pl.when(c > 0)
    def _():
        back_copy(0).wait_send()
        back_copy(1).wait_send()

    for j in range(m):

        @pl.when(h * m + j != c)
        def _():
            x_copy(j, 0).wait_send()

        x_copy(j, 1).wait_send()

    state_copy().wait_send()

    @pl.when(c >= 2)
    def _():
        chain().wait_send()

    for p in range(2):

        @pl.when(roots[p])
        def _():
            for i in range(n):
                slot = lax.rem(c + i, n)
                forward(p, slot, 3 * i, across).wait_send()
                forward(p, slot, 3 * i + 1, sibling).wait_send()
                forward(1 - p, slot, 3 * i + 2, sibling).wait_send()

    share(sent)
    spread(sent, False)


def fused(layer_input, queries, keys, values, result_cotangent, log_decay):
    n = lax.axis_size("ctx")
    length, width = layer_input.shape
    rows = width * lax.axis_size("head") // n
    m = width // rows
    dma = pltpu.SemaphoreType.DMA
    shape = jax.ShapeDtypeStruct((rows, E), BF16)
    vmem = pl.BlockSpec(memory_space=pltpu.VMEM)
    return pl.pallas_call(
        functools.partial(fused_kernel, n, m),
        out_shape=(shape, shape),
        in_specs=[pl.BlockSpec(memory_space=pltpu.HBM)] * 6,
        out_specs=(vmem, vmem),
        scratch_shapes=[
            pltpu.VMEM(queries.shape, BF16),
            pltpu.VMEM(keys.shape, BF16),
            pltpu.VMEM(values.shape, BF16),
            pltpu.VMEM(queries.shape, BF16),
            pltpu.VMEM(log_decay.shape, F32),
            dma((5,)),
            pltpu.VMEM((2, n, length // 2, rows), BF16),
            pltpu.VMEM((2, n, length, E), BF16),
            pltpu.VMEM((n, E + 32, E), BF16),
            pltpu.VMEM((2, length, E), BF16),
            pltpu.VMEM((2, length, E), BF16),
            pltpu.VMEM((2, length, E), BF16),
            pltpu.VMEM((length, E), F32),
            pltpu.VMEM((length, E), F32),
            pltpu.VMEM((E, E), F32),
            pltpu.VMEM((E, E), F32),
            pltpu.VMEM((E, E), F32),
            dma((m, 2)),
            dma((2, n)),
            dma,
            dma((3 * n,)),
            dma((2, n)),
            dma((2, n)),
            dma((2, n)),
            dma((2, n)),
            dma((2,)),
            dma((n + 1,)),
            dma((2,)),
            dma((2,)),
            dma((2,)),
            dma((2,)),
        ],
        compiler_params=pltpu.CompilerParams(
            collective_id=0, has_side_effects=True, vmem_limit_bytes=60 * 1024 * 1024
        ),
    )(layer_input, queries, keys, values, result_cotangent, log_decay)


def solution(mesh):
    in_specs = (
        P("ctx", "head"),
        P("ctx", "head"),
        P("ctx", "head"),
        P("ctx", "head"),
        P("ctx", "head"),
        P("head", "ctx"),
    )
    out_specs = (P("ctx", "head"), P("ctx", "head"))
    n, heads = mesh.shape["ctx"], mesh.shape["head"]

    def body(*args):
        return (fused if fits(args, n, heads) else on_device)(*args)

    return jax.shard_map(
        body, mesh=mesh, in_specs=in_specs, out_specs=out_specs, check_vma=False
    )
```

```python
import functools

import jax
import jax.numpy as jnp
from jax import lax
from jax.experimental import pallas as pl
from jax.experimental.pallas import tpu as pltpu
from jax.sharding import PartitionSpec as P

E = 128
WINDOW = 256


neg_fill = -1e30


def entering(array, axis, combine, identity):
    size, position = (lax.axis_size(axis), lax.axis_index(axis))
    everything = jax.tree.map(lambda part: lax.all_gather(part, axis), array)
    start = jax.tree.map(
        lambda part, zero: jnp.broadcast_to(jnp.asarray(zero, part.dtype), part.shape),
        array,
        identity,
    )

    def turn(k, before):
        at = size - 1 - k
        reached = at > position
        new = combine(before, jax.tree.map(lambda part: part[at], everything))
        return jax.tree.map(lambda a, b: jnp.where(reached, a, b), new, before)

    return lax.fori_loop(0, size, turn, start)


def shifted(value, axis, steps):
    count = lax.axis_size(axis)
    leading, last = (max(0, -steps), min(count, count - steps))
    return lax.ppermute(value, axis, [(source, source + steps) for source in range(leading, last)])


def band_grads(q_block, h_block, key_rows, value_rows, query_pos, key_pos):
    head_dim = key_rows.shape[1]
    group_size = q_block.shape[1] // head_dim
    row_count = q_block.shape[0]
    q_heads = q_block.reshape(row_count, group_size, head_dim)
    h_heads = h_block.reshape(row_count, group_size, head_dim)
    factor = head_dim ** (-0.5)
    scores = (
        jnp.einsum("trd,jd->rtj", q_heads, key_rows, preferred_element_type=jnp.float32) * factor
    )
    offset = query_pos[:, None] - key_pos[None, :]
    inside = (offset >= 0) & (offset < WINDOW) & (key_pos[None, :] >= 0)
    scores = jnp.where(inside[None], scores, neg_fill)
    row_max = jnp.max(scores, axis=2, keepdims=True)
    expo = jnp.exp(scores - row_max)
    attend = expo / jnp.sum(expo, axis=2, keepdims=True)
    attend_low = attend.astype(jnp.bfloat16)
    dprob = jnp.einsum("trd,jd->rtj", h_heads, value_rows, preferred_element_type=jnp.float32)
    row_delta = jnp.sum(attend * dprob, axis=2, keepdims=True)
    dscore = (attend * (dprob - row_delta)).astype(jnp.bfloat16)
    key_part = (
        jnp.einsum("rtj,trd->jd", dscore, q_heads, preferred_element_type=jnp.float32) * factor
    )
    value_part = jnp.einsum("rtj,trd->jd", attend_low, h_heads, preferred_element_type=jnp.float32)
    return (key_part, value_part)


def linear_terms(q_block, h_block, key_rows, value_rows, log_rates, lin_scale):
    head_dim = key_rows.shape[1]
    group_size = q_block.shape[1] // head_dim
    length = q_block.shape[0]
    q_heads = q_block.reshape(length, group_size, head_dim)
    h_heads = h_block.reshape(length, group_size, head_dim)
    row_after = lax.broadcasted_iota(jnp.int32, (length, length), 0)
    row_before = lax.broadcasted_iota(jnp.int32, (length, length), 1)
    log_sums = jnp.sum(jnp.where(row_after >= row_before, log_rates[None, :], 0.0), axis=1)
    mixing = jnp.exp(
        jnp.where(row_after >= row_before, log_sums[:, None] - log_sums[None, :], neg_fill)
    )
    key_mix = (
        mixing[None]
        * jnp.einsum("trd,jd->rtj", h_heads, value_rows, preferred_element_type=jnp.float32)
    ).astype(jnp.bfloat16)
    value_mix = (
        mixing[None]
        * jnp.einsum("trd,jd->rtj", q_heads, key_rows, preferred_element_type=jnp.float32)
    ).astype(jnp.bfloat16)
    key_part = (
        jnp.einsum("rtj,trd->jd", key_mix, q_heads, preferred_element_type=jnp.float32) * lin_scale
    )
    value_part = (
        jnp.einsum("rtj,trd->jd", value_mix, h_heads, preferred_element_type=jnp.float32)
        * lin_scale
    )
    weighted = (jnp.exp(log_sums)[:, None, None] * h_heads).astype(jnp.bfloat16)
    block_grad = (
        jnp.einsum("trd,tre->de", q_heads, weighted, preferred_element_type=jnp.float32) * lin_scale
    )
    return (
        key_part,
        value_part,
        block_grad,
        jnp.exp(log_sums[-1]),
        jnp.exp(log_sums[-1] - log_sums),
    )


def compose(earlier, later):
    return (later[0] * earlier[0], later[0][:, None, None] * earlier[1] + later[1])


def on_device(layer_input, queries, keys, values, result_cotangent, log_decay):
    length = queries.shape[0]
    head_dim = E
    lin_scale = 1.0 / (32 * head_dim)
    halves = result_cotangent * 0.5
    row_start = lax.axis_index("ctx") * length
    query_pos = row_start + jnp.arange(length, dtype=jnp.int32)
    key_pos = row_start - WINDOW + jnp.arange(length + WINDOW, dtype=jnp.int32)
    linear_parts = [linear_terms(queries, halves, keys, values, log_decay[0], lin_scale)]
    decays = jnp.stack([part[3] for part in linear_parts])
    block_grads = jnp.stack([part[2] for part in linear_parts])
    identity = (jnp.ones_like(decays), jnp.zeros_like(block_grads))
    _, incoming = entering((decays, block_grads), "ctx", compose, identity)
    preceding_keys, prior_v = shifted((keys, values), "ctx", 1)
    full_k = jnp.concatenate([preceding_keys, keys], axis=0)
    full_v = jnp.concatenate([prior_v, values], axis=0)
    band_parts = [band_grads(queries, halves, full_k, full_v, query_pos, key_pos)]
    win_k = jnp.concatenate([part[0] for part in band_parts], axis=1)
    win_v = jnp.concatenate([part[1] for part in band_parts], axis=1)
    back_k, back_v = shifted((win_k[:WINDOW], win_v[:WINDOW]), "ctx", -1)
    win_k = win_k[WINDOW:]
    win_v = win_v[WINDOW:]
    zero_rows = jnp.zeros((length - WINDOW, win_k.shape[1]), jnp.float32)
    win_k = win_k + jnp.concatenate([zero_rows, back_k], axis=0)
    win_v = win_v + jnp.concatenate([zero_rows, back_v], axis=0)
    state_in = incoming[0]
    tail_decay = linear_parts[0][4][:, None]
    lin_keys = linear_parts[0][0] + tail_decay * jnp.dot(
        values.astype(jnp.float32), state_in.T, precision=lax.Precision.HIGHEST
    )
    lin_values = linear_parts[0][1] + tail_decay * jnp.dot(
        keys.astype(jnp.float32), state_in, precision=lax.Precision.HIGHEST
    )
    key_grad = (lin_keys + win_k).astype(jnp.bfloat16)
    value_grad = (lin_values + win_v).astype(jnp.bfloat16)
    both_grads = jnp.concatenate([key_grad, value_grad], axis=1)
    partial_value = lax.dot_general(
        lax.all_gather(layer_input, "head", axis=1, tiled=True),
        both_grads,
        (((0,), (0,)), ((), ())),
        preferred_element_type=jnp.float32,
    )
    owned = lax.psum_scatter(partial_value, "ctx", scatter_dimension=0, tiled=True)
    key_width = key_grad.shape[1]
    return (owned[:, :key_width].astype(jnp.bfloat16), owned[:, key_width:].astype(jnp.bfloat16))


MESH = pl.DeviceIdType.MESH
F32, BF16 = jnp.float32, jnp.bfloat16


def fits(args, n, heads):
    x, q, k = args[0], args[1], args[2]
    rows = x.shape[1] * heads // n
    return (
        heads == 4
        and n == 2 * heads
        and rows % 128 == 0
        and x.shape[0] == WINDOW
        and k.shape[1] == E
        and q.shape[1] % E == 0
        and x.shape[1] == 2 * rows
    )


def tn(a, b):
    return lax.dot_general(a, b, (((0,), (0,)), ((), ())), preferred_element_type=F32)


def nt(a, b):
    return lax.dot_general(a, b, (((1,), (1,)), ((), ())), preferred_element_type=F32)


def fused_kernel(
    n, m, x_ref, q_hbm, k_hbm, v_hbm, d_hbm, ld_hbm, ok_ref, ov_ref,
    q_ref, k_ref, v_ref, d_ref, ld_ref, in_sem, xall, gall, sall, halo, back_out, back_in, part_k, part_v, state, chain_out, chain_in,
    x_send, x_recv, x_own, f_send, g_up, g_down, g_side, g_recv, s_send, s_recv, h_send, h_recv, b_send, b_recv,
):
    length, width = q_ref.shape
    group = width // E
    rows = x_ref.shape[1] // m
    part = length // 2
    factor = E ** (-0.5)
    lin_scale = 1.0 / (32 * E)
    c, h = lax.axis_index("ctx"), lax.axis_index("head")
    owner = c // m
    sibling = h + 1 - 2 * lax.rem(h, 2)
    across = lax.rem(h + 2, 4)

    def copy(src, dst, send, recv, ctx, head):
        return pltpu.make_async_remote_copy(
            src_ref=src, dst_ref=dst, send_sem=send, recv_sem=recv,
            device_id=(ctx, head), device_id_type=MESH,
        )

    loads = [
        pltpu.make_async_copy(src, dst, in_sem.at[i])
        for i, (src, dst) in enumerate(
            ((ld_hbm, ld_ref), (q_hbm, q_ref), (d_hbm, d_ref), (k_hbm, k_ref), (v_hbm, v_ref))
        )
    ]
    for load in loads:
        load.start()

    peers = [lax.rem(c + i, n) for i in range(1, n)]
    barrier = pltpu.get_barrier_semaphore()
    for p in peers:
        pl.semaphore_signal(barrier, inc=1, device_id=(p, h), device_id_type=MESH)
        pl.semaphore_signal(barrier, inc=1, device_id=(p, across), device_id_type=MESH)
    for i in range(1, 4):
        pl.semaphore_signal(
            barrier, inc=1, device_id=(c, lax.rem(h + i, 4)), device_id_type=MESH
        )
    pl.semaphore_wait(barrier, 2 * n + 1)

    def halo_copy(i):
        return copy(
            (k_hbm, v_hbm)[i], halo.at[i], h_send.at[i], h_recv.at[i], lax.rem(c + 1, n), h
        )

    @pl.when(c < n - 1)
    def _():
        halo_copy(0).start()
        halo_copy(1).start()

    @pl.when(c == 0)
    def _():
        halo[...] = jnp.zeros_like(halo)

    def x_copy(j, p):
        return copy(
            x_ref.at[pl.ds(p * part, part), pl.ds(j * rows, rows)], xall.at[p, c],
            x_send.at[j, p], x_recv.at[p, c], h * m + j, (h, across)[p],
        )

    def x_local(j):
        return pltpu.make_async_copy(
            x_ref.at[pl.ds(0, part), pl.ds(j * rows, rows)], xall.at[0, c], x_own
        )

    for j in range(m):

        @pl.when(h * m + j == c)
        def _():
            x_local(j).start()

        @pl.when(h * m + j != c)
        def _():
            x_copy(j, 0).start()

        x_copy(j, 1).start()

    for load in loads:
        load.wait()

    after = lax.broadcasted_iota(jnp.int32, (length, length), 0)
    before = lax.broadcasted_iota(jnp.int32, (length, length), 1)
    lower = after >= before
    sums = jnp.sum(jnp.where(lower, ld_ref[...], 0.0), axis=1, keepdims=True)
    sums_row = jnp.sum(jnp.where(after == before, sums, 0.0), axis=0, keepdims=True)
    total = jnp.sum(ld_ref[...], axis=1, keepdims=True)

    grown = jnp.exp(sums)
    qs, hs, grad = [], [], jnp.zeros((E, E), F32)
    for r in range(group):
        qs.append(q_ref[:, r * E : (r + 1) * E])
        hs.append((d_ref[:, r * E : (r + 1) * E].astype(F32) * 0.5).astype(BF16))
        grad += tn(qs[r], (grown * hs[r].astype(F32)).astype(BF16))
    decay = jnp.broadcast_to(jnp.exp(total), (16, E))
    coarse = decay.astype(BF16)
    fine = (decay - coarse.astype(F32)).astype(BF16)
    sall[c, 0:E, :] = (grad * lin_scale).astype(BF16)
    sall[c, E : E + 16, :] = coarse
    sall[c, E + 16 : E + 32, :] = fine

    side = c + 1 - 2 * lax.rem(c, 2)

    def state_copy():
        return copy(sall.at[c], sall.at[c], s_send.at[0], s_recv.at[c], side, h)

    state_copy().start()

    mixing = jnp.exp(jnp.where(lower, sums - sums_row, neg_fill))
    keys, vals = k_ref[...], v_ref[...]
    lin_k = jnp.zeros((length, E), F32)
    lin_v = jnp.zeros((length, E), F32)
    own_s, own_p = [], []
    for r in range(group):
        own_s.append(nt(qs[r], keys))
        own_p.append(nt(hs[r], vals))
        lin_k += tn((mixing * own_p[r]).astype(BF16), qs[r])
        lin_v += tn((mixing * own_s[r]).astype(BF16), hs[r])

    def chain():
        return copy(chain_out, chain_in, s_send.at[1], s_recv.at[n], lax.rem(c + n - 2, n), h)

    def enter():
        copy(sall.at[side], sall.at[side], s_send.at[0], s_recv.at[side], side, h).wait_recv()

        @pl.when(c >= n - 2)
        def _():
            chain_in[...] = jnp.zeros_like(chain_in)

        @pl.when(c < n - 2)
        def _():
            chain().wait_recv()

        def through(slot, later):
            kept = sall[slot, E : E + 1, :].astype(F32) + sall[slot, E + 16 : E + 17, :].astype(F32)
            return kept * later + sall[slot, 0:E, :].astype(F32)

        first = c - lax.rem(c, 2)
        beyond = chain_in[...].astype(F32)
        between = through(first + 1, beyond)

        @pl.when(c >= 2)
        def _():
            chain_out[...] = through(first, between).astype(BF16)
            chain().start()

        state[...] = jnp.where(c == first, between, beyond)

    @pl.when(c >= n // 2)
    def _():
        enter()

    @pl.when(c > 0)
    def _():
        halo_copy(0).wait_recv()
        halo_copy(1).wait_recv()

    old_k, old_v = halo[0], halo[1]
    upper = jnp.logical_and(before > after, c > 0)
    win = [jnp.zeros((length, E), F32) for _ in range(4)]
    for r in range(group):
        s_own = jnp.where(lower, own_s[r] * factor, neg_fill)
        s_old = jnp.where(upper, nt(qs[r], old_k) * factor, neg_fill)
        top = jnp.maximum(
            jnp.max(s_own, axis=1, keepdims=True), jnp.max(s_old, axis=1, keepdims=True)
        )
        e_own, e_old = jnp.exp(s_own - top), jnp.exp(s_old - top)
        inv = 1.0 / (jnp.sum(e_own, axis=1, keepdims=True) + jnp.sum(e_old, axis=1, keepdims=True))
        a_own, a_old = e_own * inv, e_old * inv
        p_old = nt(hs[r], old_v)
        delta = jnp.sum(a_own * own_p[r], axis=1, keepdims=True) + jnp.sum(
            a_old * p_old, axis=1, keepdims=True
        )
        win[0] += tn((a_old * (p_old - delta)).astype(BF16), qs[r])
        win[1] += tn(a_old.astype(BF16), hs[r])
        win[2] += tn((a_own * (own_p[r] - delta)).astype(BF16), qs[r])
        win[3] += tn(a_own.astype(BF16), hs[r])
    back_out[0] = (win[0] * factor).astype(BF16)
    back_out[1] = win[1].astype(BF16)

    def back_copy(i):
        return copy(
            back_out.at[i], back_in.at[i], b_send.at[i], b_recv.at[i], lax.rem(c + n - 1, n), h
        )

    @pl.when(c > 0)
    def _():
        back_copy(0).start()
        back_copy(1).start()

    part_k[...] = lin_k * lin_scale + win[2] * factor
    part_v[...] = lin_v * lin_scale + win[3]

    def forward(p, slot, i, head):
        return copy(xall.at[p, slot], xall.at[p, slot], f_send.at[i], x_recv.at[p, slot], c, head)

    def arrived(p, slot):
        return copy(
            xall.at[p, slot], xall.at[p, slot], x_send.at[0, 0], x_recv.at[p, slot], c, sibling
        )

    roots = (h == owner, across == owner)
    @pl.when(c < n // 2)
    def _():
        enter()

    high = state[...].astype(BF16)
    low = (state[...] - high.astype(F32)).astype(BF16)
    ending = jnp.exp(total - sums)
    part_k[...] += ending * (nt(vals, high) + nt(vals, low))
    part_v[...] += ending * (
        jnp.dot(keys, high, preferred_element_type=F32)
        + jnp.dot(keys, low, preferred_element_type=F32)
    )

    @pl.when(c < n - 1)
    def _():
        back_copy(0).wait_recv()
        back_copy(1).wait_recv()
        part_k[...] += back_in[0].astype(F32)
        part_v[...] += back_in[1].astype(F32)

    gall[0, c] = part_k[...].astype(BF16)
    gall[1, c] = part_v[...].astype(BF16)

    up_ok, down_ok = c < n - 2, c >= 2

    def up(p, slot):
        return copy(gall.at[p, slot], gall.at[p, slot], g_up.at[p, slot], g_recv.at[p, slot], lax.rem(c + 2, n), h)

    def down(p, slot):
        return copy(gall.at[p, slot], gall.at[p, slot], g_down.at[p, slot], g_recv.at[p, slot], lax.rem(c + n - 2, n), h)

    def beside(p, slot):
        return copy(gall.at[p, slot], gall.at[p, slot], g_side.at[p, slot], g_recv.at[p, slot], side, h)

    def along(act, p, slot, upward, downward):
        if upward:

            @pl.when(up_ok)
            def _():
                act(up(p, slot))

        if downward:

            @pl.when(down_ok)
            def _():
                act(down(p, slot))

    def start(dma):
        dma.start()

    def sent(dma):
        dma.wait_send()

    def arrive(p, slot):
        beside(p, slot).wait_recv()

    def share(act):
        act(beside(0, c))
        along(act, 0, c, True, True)
        along(act, 1, c, True, True)
        act(beside(1, c))

    def spread(act, wait):
        if wait:
            arrive(0, side)
        along(act, 0, side, True, True)
        for d in range(2, n, 2):

            @pl.when(c - d >= 0)
            def _():
                for p, slot in ((0, c - d), (1, c - d), (0, side - d)):
                    if wait:
                        arrive(p, slot)
                    along(act, p, slot, True, False)
                    if p:
                        act(beside(p, slot))

            @pl.when(c + d < n)
            def _():
                for p, slot in ((0, c + d), (1, c + d), (0, side + d)):
                    if wait:
                        arrive(p, slot)
                    along(act, p, slot, False, True)
                    if p:
                        act(beside(p, slot))

    share(start)

    for p in range(2):

        @pl.when(roots[p])
        def _():
            for i in range(n - 1, -1, -1):
                slot = lax.rem(c + i, n)
                if i or p:
                    arrived(p, slot).wait_recv()
                else:
                    x_local(0).wait()
                forward(p, slot, 3 * i, across).start()
                forward(p, slot, 3 * i + 1, sibling).start()

    spread(start, True)

    for p in range(2):

        @pl.when(roots[1 - p])
        def _():
            for i in range(n - 1, -1, -1):
                slot = lax.rem(c + i, n)
                arrived(p, slot).wait_recv()
                forward(p, slot, 3 * i + 2, sibling).start()

    @pl.when(lax.rem(h + owner, 2) == 1)
    def _():
        for slot in range(n):
            arrived(0, slot).wait_recv()
            arrived(1, slot).wait_recv()

    for i in range(0, n, 2):
        slot = lax.rem(side + i, n)
        arrive(1, slot)
    acc_k = jnp.zeros((rows, E), F32)
    acc_v = jnp.zeros((rows, E), F32)
    for slot in range(n):
        both = xall[:, slot].reshape(length, rows)
        acc_k += tn(both, gall[0, slot])
        acc_v += tn(both, gall[1, slot])
    ok_ref[...] = acc_k.astype(BF16)
    ov_ref[...] = acc_v.astype(BF16)

    @pl.when(c < n - 1)
    def _():
        halo_copy(0).wait_send()
        halo_copy(1).wait_send()

    @pl.when(c > 0)
    def _():
        back_copy(0).wait_send()
        back_copy(1).wait_send()

    for j in range(m):

        @pl.when(h * m + j != c)
        def _():
            x_copy(j, 0).wait_send()

        x_copy(j, 1).wait_send()

    state_copy().wait_send()

    @pl.when(c >= 2)
    def _():
        chain().wait_send()

    for p in range(2):

        @pl.when(roots[p])
        def _():
            for i in range(n):
                slot = lax.rem(c + i, n)
                forward(p, slot, 3 * i, across).wait_send()
                forward(p, slot, 3 * i + 1, sibling).wait_send()
                forward(1 - p, slot, 3 * i + 2, sibling).wait_send()

    share(sent)
    spread(sent, False)


def fused(layer_input, queries, keys, values, result_cotangent, log_decay):
    n = lax.axis_size("ctx")
    length, width = layer_input.shape
    rows = width * lax.axis_size("head") // n
    m = width // rows
    dma = pltpu.SemaphoreType.DMA
    shape = jax.ShapeDtypeStruct((rows, E), BF16)
    vmem = pl.BlockSpec(memory_space=pltpu.VMEM)
    return pl.pallas_call(
        functools.partial(fused_kernel, n, m),
        out_shape=(shape, shape),
        in_specs=[pl.BlockSpec(memory_space=pltpu.HBM)] * 6,
        out_specs=(vmem, vmem),
        scratch_shapes=[
            pltpu.VMEM(queries.shape, BF16),
            pltpu.VMEM(keys.shape, BF16),
            pltpu.VMEM(values.shape, BF16),
            pltpu.VMEM(queries.shape, BF16),
            pltpu.VMEM(log_decay.shape, F32),
            dma((5,)),
            pltpu.VMEM((2, n, length // 2, rows), BF16),
            pltpu.VMEM((2, n, length, E), BF16),
            pltpu.VMEM((n, E + 32, E), BF16),
            pltpu.VMEM((2, length, E), BF16),
            pltpu.VMEM((2, length, E), BF16),
            pltpu.VMEM((2, length, E), BF16),
            pltpu.VMEM((length, E), F32),
            pltpu.VMEM((length, E), F32),
            pltpu.VMEM((E, E), F32),
            pltpu.VMEM((E, E), BF16),
            pltpu.VMEM((E, E), BF16),
            dma((m, 2)),
            dma((2, n)),
            dma,
            dma((3 * n,)),
            dma((2, n)),
            dma((2, n)),
            dma((2, n)),
            dma((2, n)),
            dma((2,)),
            dma((n + 1,)),
            dma((2,)),
            dma((2,)),
            dma((2,)),
            dma((2,)),
        ],
        compiler_params=pltpu.CompilerParams(
            collective_id=0, has_side_effects=True, vmem_limit_bytes=60 * 1024 * 1024
        ),
    )(layer_input, queries, keys, values, result_cotangent, log_decay)


def solution(mesh):
    in_specs = (
        P("ctx", "head"),
        P("ctx", "head"),
        P("ctx", "head"),
        P("ctx", "head"),
        P("ctx", "head"),
        P("head", "ctx"),
    )
    out_specs = (P("ctx", "head"), P("ctx", "head"))
    n, heads = mesh.shape["ctx"], mesh.shape["head"]

    def body(*args):
        return (fused if fits(args, n, heads) else on_device)(*args)

    return jax.shard_map(
        body, mesh=mesh, in_specs=in_specs, out_specs=out_specs, check_vma=False
    )
```

```python
import functools

import jax
import jax.numpy as jnp
from jax import lax
from jax.experimental import pallas as pl
from jax.experimental.pallas import tpu as pltpu
from jax.sharding import PartitionSpec as P

E = 128
WINDOW = 256


neg_fill = -1e30


def entering(array, axis, combine, identity):
    size, position = (lax.axis_size(axis), lax.axis_index(axis))
    everything = jax.tree.map(lambda part: lax.all_gather(part, axis), array)
    start = jax.tree.map(
        lambda part, zero: jnp.broadcast_to(jnp.asarray(zero, part.dtype), part.shape),
        array,
        identity,
    )

    def turn(k, before):
        at = size - 1 - k
        reached = at > position
        new = combine(before, jax.tree.map(lambda part: part[at], everything))
        return jax.tree.map(lambda a, b: jnp.where(reached, a, b), new, before)

    return lax.fori_loop(0, size, turn, start)


def shifted(value, axis, steps):
    count = lax.axis_size(axis)
    leading, last = (max(0, -steps), min(count, count - steps))
    return lax.ppermute(value, axis, [(source, source + steps) for source in range(leading, last)])


def band_grads(q_block, h_block, key_rows, value_rows, query_pos, key_pos):
    head_dim = key_rows.shape[1]
    group_size = q_block.shape[1] // head_dim
    row_count = q_block.shape[0]
    q_heads = q_block.reshape(row_count, group_size, head_dim)
    h_heads = h_block.reshape(row_count, group_size, head_dim)
    factor = head_dim ** (-0.5)
    scores = (
        jnp.einsum("trd,jd->rtj", q_heads, key_rows, preferred_element_type=jnp.float32) * factor
    )
    offset = query_pos[:, None] - key_pos[None, :]
    inside = (offset >= 0) & (offset < WINDOW) & (key_pos[None, :] >= 0)
    scores = jnp.where(inside[None], scores, neg_fill)
    row_max = jnp.max(scores, axis=2, keepdims=True)
    expo = jnp.exp(scores - row_max)
    attend = expo / jnp.sum(expo, axis=2, keepdims=True)
    attend_low = attend.astype(jnp.bfloat16)
    dprob = jnp.einsum("trd,jd->rtj", h_heads, value_rows, preferred_element_type=jnp.float32)
    row_delta = jnp.sum(attend * dprob, axis=2, keepdims=True)
    dscore = (attend * (dprob - row_delta)).astype(jnp.bfloat16)
    key_part = (
        jnp.einsum("rtj,trd->jd", dscore, q_heads, preferred_element_type=jnp.float32) * factor
    )
    value_part = jnp.einsum("rtj,trd->jd", attend_low, h_heads, preferred_element_type=jnp.float32)
    return (key_part, value_part)


def linear_terms(q_block, h_block, key_rows, value_rows, log_rates, lin_scale):
    head_dim = key_rows.shape[1]
    group_size = q_block.shape[1] // head_dim
    length = q_block.shape[0]
    q_heads = q_block.reshape(length, group_size, head_dim)
    h_heads = h_block.reshape(length, group_size, head_dim)
    row_after = lax.broadcasted_iota(jnp.int32, (length, length), 0)
    row_before = lax.broadcasted_iota(jnp.int32, (length, length), 1)
    log_sums = jnp.sum(jnp.where(row_after >= row_before, log_rates[None, :], 0.0), axis=1)
    mixing = jnp.exp(
        jnp.where(row_after >= row_before, log_sums[:, None] - log_sums[None, :], neg_fill)
    )
    key_mix = (
        mixing[None]
        * jnp.einsum("trd,jd->rtj", h_heads, value_rows, preferred_element_type=jnp.float32)
    ).astype(jnp.bfloat16)
    value_mix = (
        mixing[None]
        * jnp.einsum("trd,jd->rtj", q_heads, key_rows, preferred_element_type=jnp.float32)
    ).astype(jnp.bfloat16)
    key_part = (
        jnp.einsum("rtj,trd->jd", key_mix, q_heads, preferred_element_type=jnp.float32) * lin_scale
    )
    value_part = (
        jnp.einsum("rtj,trd->jd", value_mix, h_heads, preferred_element_type=jnp.float32)
        * lin_scale
    )
    weighted = (jnp.exp(log_sums)[:, None, None] * h_heads).astype(jnp.bfloat16)
    block_grad = (
        jnp.einsum("trd,tre->de", q_heads, weighted, preferred_element_type=jnp.float32) * lin_scale
    )
    return (
        key_part,
        value_part,
        block_grad,
        jnp.exp(log_sums[-1]),
        jnp.exp(log_sums[-1] - log_sums),
    )


def compose(earlier, later):
    return (later[0] * earlier[0], later[0][:, None, None] * earlier[1] + later[1])


def on_device(layer_input, queries, keys, values, result_cotangent, log_decay):
    length = queries.shape[0]
    head_dim = E
    lin_scale = 1.0 / (32 * head_dim)
    halves = result_cotangent * 0.5
    row_start = lax.axis_index("ctx") * length
    query_pos = row_start + jnp.arange(length, dtype=jnp.int32)
    key_pos = row_start - WINDOW + jnp.arange(length + WINDOW, dtype=jnp.int32)
    linear_parts = [linear_terms(queries, halves, keys, values, log_decay[0], lin_scale)]
    decays = jnp.stack([part[3] for part in linear_parts])
    block_grads = jnp.stack([part[2] for part in linear_parts])
    identity = (jnp.ones_like(decays), jnp.zeros_like(block_grads))
    _, incoming = entering((decays, block_grads), "ctx", compose, identity)
    preceding_keys, prior_v = shifted((keys, values), "ctx", 1)
    full_k = jnp.concatenate([preceding_keys, keys], axis=0)
    full_v = jnp.concatenate([prior_v, values], axis=0)
    band_parts = [band_grads(queries, halves, full_k, full_v, query_pos, key_pos)]
    win_k = jnp.concatenate([part[0] for part in band_parts], axis=1)
    win_v = jnp.concatenate([part[1] for part in band_parts], axis=1)
    back_k, back_v = shifted((win_k[:WINDOW], win_v[:WINDOW]), "ctx", -1)
    win_k = win_k[WINDOW:]
    win_v = win_v[WINDOW:]
    zero_rows = jnp.zeros((length - WINDOW, win_k.shape[1]), jnp.float32)
    win_k = win_k + jnp.concatenate([zero_rows, back_k], axis=0)
    win_v = win_v + jnp.concatenate([zero_rows, back_v], axis=0)
    state_in = incoming[0]
    tail_decay = linear_parts[0][4][:, None]
    lin_keys = linear_parts[0][0] + tail_decay * jnp.dot(
        values.astype(jnp.float32), state_in.T, precision=lax.Precision.HIGHEST
    )
    lin_values = linear_parts[0][1] + tail_decay * jnp.dot(
        keys.astype(jnp.float32), state_in, precision=lax.Precision.HIGHEST
    )
    key_grad = (lin_keys + win_k).astype(jnp.bfloat16)
    value_grad = (lin_values + win_v).astype(jnp.bfloat16)
    both_grads = jnp.concatenate([key_grad, value_grad], axis=1)
    partial_value = lax.dot_general(
        lax.all_gather(layer_input, "head", axis=1, tiled=True),
        both_grads,
        (((0,), (0,)), ((), ())),
        preferred_element_type=jnp.float32,
    )
    owned = lax.psum_scatter(partial_value, "ctx", scatter_dimension=0, tiled=True)
    key_width = key_grad.shape[1]
    return (owned[:, :key_width].astype(jnp.bfloat16), owned[:, key_width:].astype(jnp.bfloat16))


MESH = pl.DeviceIdType.MESH
F32, BF16 = jnp.float32, jnp.bfloat16


def fits(args, n, heads):
    x, q, k = args[0], args[1], args[2]
    rows = x.shape[1] * heads // n
    return (
        heads == 4
        and n == 2 * heads
        and rows % 128 == 0
        and x.shape[0] == WINDOW
        and k.shape[1] == E
        and q.shape[1] % E == 0
        and x.shape[1] == 2 * rows
    )


def tn(a, b):
    return lax.dot_general(a, b, (((0,), (0,)), ((), ())), preferred_element_type=F32)


def nt(a, b):
    return lax.dot_general(a, b, (((1,), (1,)), ((), ())), preferred_element_type=F32)


def fused_kernel(
    n, m, x_ref, q_hbm, k_hbm, v_hbm, d_hbm, ld_hbm, ok_ref, ov_ref,
    q_ref, k_ref, v_ref, d_ref, ld_ref, in_sem, xall, gall, sall, halo, back_out, back_in, part_k, part_v, state, chain_out, chain_in,
    x_send, x_recv, x_own, f_send, g_up, g_down, g_side, g_recv, s_send, s_recv, h_send, h_recv, b_send, b_recv,
):
    length, width = q_ref.shape
    group = width // E
    rows = x_ref.shape[1] // m
    part = length // 2
    factor = E ** (-0.5)
    lin_scale = 1.0 / (32 * E)
    c, h = lax.axis_index("ctx"), lax.axis_index("head")
    owner = c // m
    sibling = h + 1 - 2 * lax.rem(h, 2)
    across = lax.rem(h + 2, 4)

    def copy(src, dst, send, recv, ctx, head):
        return pltpu.make_async_remote_copy(
            src_ref=src, dst_ref=dst, send_sem=send, recv_sem=recv,
            device_id=(ctx, head), device_id_type=MESH,
        )

    loads = [
        pltpu.make_async_copy(src, dst, in_sem.at[i])
        for i, (src, dst) in enumerate(
            ((ld_hbm, ld_ref), (q_hbm, q_ref), (d_hbm, d_ref), (k_hbm, k_ref), (v_hbm, v_ref))
        )
    ]
    for load in loads:
        load.start()

    peers = [lax.rem(c + i, n) for i in range(1, n)]
    barrier = pltpu.get_barrier_semaphore()
    for p in peers:
        pl.semaphore_signal(barrier, inc=1, device_id=(p, h), device_id_type=MESH)
        pl.semaphore_signal(barrier, inc=1, device_id=(p, across), device_id_type=MESH)
    for i in range(1, 4):
        pl.semaphore_signal(
            barrier, inc=1, device_id=(c, lax.rem(h + i, 4)), device_id_type=MESH
        )
    pl.semaphore_wait(barrier, 2 * n + 1)

    def halo_copy(i):
        return copy(
            (k_hbm, v_hbm)[i], halo.at[i], h_send.at[i], h_recv.at[i], lax.rem(c + 1, n), h
        )

    @pl.when(c < n - 1)
    def _():
        halo_copy(0).start()
        halo_copy(1).start()

    @pl.when(c == 0)
    def _():
        halo[...] = jnp.zeros_like(halo)

    def x_copy(j, p):
        return copy(
            x_ref.at[pl.ds(p * part, part), pl.ds(j * rows, rows)], xall.at[p, c],
            x_send.at[j, p], x_recv.at[p, c], h * m + j, (h, across)[p],
        )

    def x_local(j):
        return pltpu.make_async_copy(
            x_ref.at[pl.ds(0, part), pl.ds(j * rows, rows)], xall.at[0, c], x_own
        )

    for j in range(m):

        @pl.when(h * m + j == c)
        def _():
            x_local(j).start()

        @pl.when(h * m + j != c)
        def _():
            x_copy(j, 0).start()

        x_copy(j, 1).start()

    for load in loads:
        load.wait()

    after = lax.broadcasted_iota(jnp.int32, (length, length), 0)
    before = lax.broadcasted_iota(jnp.int32, (length, length), 1)
    lower = after >= before
    sums = jnp.sum(jnp.where(lower, ld_ref[...], 0.0), axis=1, keepdims=True)
    sums_row = jnp.sum(jnp.where(after == before, sums, 0.0), axis=0, keepdims=True)
    total = jnp.sum(ld_ref[...], axis=1, keepdims=True)

    grown = jnp.exp(sums)
    qs, hs, grad = [], [], jnp.zeros((E, E), F32)
    for r in range(group):
        qs.append(q_ref[:, r * E : (r + 1) * E])
        hs.append((d_ref[:, r * E : (r + 1) * E].astype(F32) * 0.5).astype(BF16))
        grad += tn(qs[r], (grown * hs[r].astype(F32)).astype(BF16))
    decay = jnp.broadcast_to(jnp.exp(total), (16, E))
    coarse = decay.astype(BF16)
    fine = (decay - coarse.astype(F32)).astype(BF16)
    sall[c, 0:E, :] = (grad * lin_scale).astype(BF16)
    sall[c, E : E + 16, :] = coarse
    sall[c, E + 16 : E + 32, :] = fine

    side = c + 1 - 2 * lax.rem(c, 2)

    def state_copy():
        return copy(sall.at[c], sall.at[c], s_send.at[0], s_recv.at[c], side, h)

    state_copy().start()

    mixing = jnp.exp(jnp.where(lower, sums - sums_row, neg_fill))
    keys, vals = k_ref[...], v_ref[...]
    lin_k = jnp.zeros((length, E), F32)
    lin_v = jnp.zeros((length, E), F32)
    own_s, own_p = [], []
    for r in range(group):
        own_s.append(nt(qs[r], keys))
        own_p.append(nt(hs[r], vals))
        lin_k += tn((mixing * own_p[r]).astype(BF16), qs[r])
        lin_v += tn((mixing * own_s[r]).astype(BF16), hs[r])

    def chain():
        return copy(chain_out, chain_in, s_send.at[1], s_recv.at[n], lax.rem(c + n - 2, n), h)

    def enter():
        copy(sall.at[side], sall.at[side], s_send.at[0], s_recv.at[side], side, h).wait_recv()

        @pl.when(c >= n - 2)
        def _():
            chain_in[...] = jnp.zeros_like(chain_in)

        @pl.when(c < n - 2)
        def _():
            chain().wait_recv()

        def through(slot, later):
            kept = sall[slot, E : E + 1, :].astype(F32) + sall[slot, E + 16 : E + 17, :].astype(F32)
            return kept * later + sall[slot, 0:E, :].astype(F32)

        first = c - lax.rem(c, 2)
        beyond = chain_in[...].astype(F32)
        between = through(first + 1, beyond)

        @pl.when(c >= 2)
        def _():
            chain_out[...] = through(first, between).astype(BF16)
            chain().start()

        state[...] = jnp.where(c == first, between, beyond)

    @pl.when(c >= n // 2)
    def _():
        enter()

    @pl.when(c > 0)
    def _():
        halo_copy(0).wait_recv()
        halo_copy(1).wait_recv()

    old_k, old_v = halo[0], halo[1]
    upper = jnp.logical_and(before > after, c > 0)
    win = [jnp.zeros((length, E), F32) for _ in range(4)]
    for r in range(group):
        s_own = jnp.where(lower, own_s[r] * factor, neg_fill)
        s_old = jnp.where(upper, nt(qs[r], old_k) * factor, neg_fill)
        top = jnp.maximum(
            jnp.max(s_own, axis=1, keepdims=True), jnp.max(s_old, axis=1, keepdims=True)
        )
        e_own, e_old = jnp.exp(s_own - top), jnp.exp(s_old - top)
        inv = 1.0 / (jnp.sum(e_own, axis=1, keepdims=True) + jnp.sum(e_old, axis=1, keepdims=True))
        a_own, a_old = e_own * inv, e_old * inv
        p_old = nt(hs[r], old_v)
        delta = jnp.sum(a_own * own_p[r], axis=1, keepdims=True) + jnp.sum(
            a_old * p_old, axis=1, keepdims=True
        )
        win[0] += tn((a_old * (p_old - delta)).astype(BF16), qs[r])
        win[1] += tn(a_old.astype(BF16), hs[r])
        win[2] += tn((a_own * (own_p[r] - delta)).astype(BF16), qs[r])
        win[3] += tn(a_own.astype(BF16), hs[r])
    back_out[0] = (win[0] * factor).astype(BF16)
    back_out[1] = win[1].astype(BF16)

    def back_copy(i):
        return copy(
            back_out.at[i], back_in.at[i], b_send.at[i], b_recv.at[i], lax.rem(c + n - 1, n), h
        )

    @pl.when(c > 0)
    def _():
        back_copy(0).start()
        back_copy(1).start()

    part_k[...] = lin_k * lin_scale + win[2] * factor
    part_v[...] = lin_v * lin_scale + win[3]

    def forward(p, slot, i, head):
        return copy(xall.at[p, slot], xall.at[p, slot], f_send.at[i], x_recv.at[p, slot], c, head)

    def arrived(p, slot):
        return copy(
            xall.at[p, slot], xall.at[p, slot], x_send.at[0, 0], x_recv.at[p, slot], c, sibling
        )

    roots = (h == owner, across == owner)
    @pl.when(c < n // 2)
    def _():
        enter()

    high = state[...].astype(BF16)
    low = (state[...] - high.astype(F32)).astype(BF16)
    ending = jnp.exp(total - sums)
    part_k[...] += ending * (nt(vals, high) + nt(vals, low))
    part_v[...] += ending * (
        jnp.dot(keys, high, preferred_element_type=F32)
        + jnp.dot(keys, low, preferred_element_type=F32)
    )

    @pl.when(c < n - 1)
    def _():
        back_copy(0).wait_recv()
        back_copy(1).wait_recv()
        part_k[...] += back_in[0].astype(F32)
        part_v[...] += back_in[1].astype(F32)

    gall[0, c] = part_k[...].astype(BF16)
    gall[1, c] = part_v[...].astype(BF16)

    up_ok, down_ok = c < n - 2, c >= 2

    def up(p, slot):
        return copy(gall.at[p, slot], gall.at[p, slot], g_up.at[p, slot], g_recv.at[p, slot], lax.rem(c + 2, n), h)

    def down(p, slot):
        return copy(gall.at[p, slot], gall.at[p, slot], g_down.at[p, slot], g_recv.at[p, slot], lax.rem(c + n - 2, n), h)

    def beside(p, slot):
        return copy(gall.at[p, slot], gall.at[p, slot], g_side.at[p, slot], g_recv.at[p, slot], side, h)

    def along(act, p, slot, upward, downward):
        if upward:

            @pl.when(up_ok)
            def _():
                act(up(p, slot))

        if downward:

            @pl.when(down_ok)
            def _():
                act(down(p, slot))

    def start(dma):
        dma.start()

    def sent(dma):
        dma.wait_send()

    def arrive(p, slot):
        beside(p, slot).wait_recv()

    def share(act):
        act(beside(0, c))
        along(act, 0, c, True, True)
        along(act, 1, c, True, True)
        act(beside(1, c))

    def hand_on():
        for p in range(2):

            @pl.when(roots[1 - p])
            def _():
                for i in range(n - 1, -1, -1):
                    slot = lax.rem(c + i, n)
                    arrived(p, slot).wait_recv()
                    forward(p, slot, 3 * i + 2, sibling).start()

    def spread(act, wait):
        if wait:
            arrive(0, side)
        along(act, 0, side, True, True)
        for d in range(2, n, 2):
            if wait and d == 4:
                hand_on()

            @pl.when(c - d >= 0)
            def _():
                for p, slot in ((0, c - d), (1, c - d), (0, side - d)):
                    if wait:
                        arrive(p, slot)
                    along(act, p, slot, True, False)
                    if p:
                        act(beside(p, slot))

            @pl.when(c + d < n)
            def _():
                for p, slot in ((0, c + d), (1, c + d), (0, side + d)):
                    if wait:
                        arrive(p, slot)
                    along(act, p, slot, False, True)
                    if p:
                        act(beside(p, slot))

    share(start)

    for p in range(2):

        @pl.when(roots[p])
        def _():
            for i in range(n - 1, -1, -1):
                slot = lax.rem(c + i, n)
                if i or p:
                    arrived(p, slot).wait_recv()
                else:
                    x_local(0).wait()
                forward(p, slot, 3 * i, across).start()
                forward(p, slot, 3 * i + 1, sibling).start()

    spread(start, True)

    @pl.when(lax.rem(h + owner, 2) == 1)
    def _():
        for slot in range(n):
            arrived(0, slot).wait_recv()
            arrived(1, slot).wait_recv()

    for i in range(0, n, 2):
        slot = lax.rem(side + i, n)
        arrive(1, slot)
    acc_k = jnp.zeros((rows, E), F32)
    acc_v = jnp.zeros((rows, E), F32)
    for slot in range(n):
        both = xall[:, slot].reshape(length, rows)
        acc_k += tn(both, gall[0, slot])
        acc_v += tn(both, gall[1, slot])
    ok_ref[...] = acc_k.astype(BF16)
    ov_ref[...] = acc_v.astype(BF16)

    @pl.when(c < n - 1)
    def _():
        halo_copy(0).wait_send()
        halo_copy(1).wait_send()

    @pl.when(c > 0)
    def _():
        back_copy(0).wait_send()
        back_copy(1).wait_send()

    for j in range(m):

        @pl.when(h * m + j != c)
        def _():
            x_copy(j, 0).wait_send()

        x_copy(j, 1).wait_send()

    state_copy().wait_send()

    @pl.when(c >= 2)
    def _():
        chain().wait_send()

    for p in range(2):

        @pl.when(roots[p])
        def _():
            for i in range(n):
                slot = lax.rem(c + i, n)
                forward(p, slot, 3 * i, across).wait_send()
                forward(p, slot, 3 * i + 1, sibling).wait_send()
                forward(1 - p, slot, 3 * i + 2, sibling).wait_send()

    share(sent)
    spread(sent, False)


def fused(layer_input, queries, keys, values, result_cotangent, log_decay):
    n = lax.axis_size("ctx")
    length, width = layer_input.shape
    rows = width * lax.axis_size("head") // n
    m = width // rows
    dma = pltpu.SemaphoreType.DMA
    shape = jax.ShapeDtypeStruct((rows, E), BF16)
    vmem = pl.BlockSpec(memory_space=pltpu.VMEM)
    return pl.pallas_call(
        functools.partial(fused_kernel, n, m),
        out_shape=(shape, shape),
        in_specs=[pl.BlockSpec(memory_space=pltpu.HBM)] * 6,
        out_specs=(vmem, vmem),
        scratch_shapes=[
            pltpu.VMEM(queries.shape, BF16),
            pltpu.VMEM(keys.shape, BF16),
            pltpu.VMEM(values.shape, BF16),
            pltpu.VMEM(queries.shape, BF16),
            pltpu.VMEM(log_decay.shape, F32),
            dma((5,)),
            pltpu.VMEM((2, n, length // 2, rows), BF16),
            pltpu.VMEM((2, n, length, E), BF16),
            pltpu.VMEM((n, E + 32, E), BF16),
            pltpu.VMEM((2, length, E), BF16),
            pltpu.VMEM((2, length, E), BF16),
            pltpu.VMEM((2, length, E), BF16),
            pltpu.VMEM((length, E), F32),
            pltpu.VMEM((length, E), F32),
            pltpu.VMEM((E, E), F32),
            pltpu.VMEM((E, E), BF16),
            pltpu.VMEM((E, E), BF16),
            dma((m, 2)),
            dma((2, n)),
            dma,
            dma((3 * n,)),
            dma((2, n)),
            dma((2, n)),
            dma((2, n)),
            dma((2, n)),
            dma((2,)),
            dma((n + 1,)),
            dma((2,)),
            dma((2,)),
            dma((2,)),
            dma((2,)),
        ],
        compiler_params=pltpu.CompilerParams(
            collective_id=0, has_side_effects=True, vmem_limit_bytes=60 * 1024 * 1024
        ),
    )(layer_input, queries, keys, values, result_cotangent, log_decay)


def solution(mesh):
    in_specs = (
        P("ctx", "head"),
        P("ctx", "head"),
        P("ctx", "head"),
        P("ctx", "head"),
        P("ctx", "head"),
        P("head", "ctx"),
    )
    out_specs = (P("ctx", "head"), P("ctx", "head"))
    n, heads = mesh.shape["ctx"], mesh.shape["head"]

    def body(*args):
        return (fused if fits(args, n, heads) else on_device)(*args)

    return jax.shard_map(
        body, mesh=mesh, in_specs=in_specs, out_specs=out_specs, check_vma=False
    )
```
